128 devices in a mesh: lat: 8 (over x, y_hi), lon: 16 (over y_lo, z, core).
Axes of the slice: x: 4, y: 4 (y_hi: 2, y_lo: 2; y = y_hi * 2 + y_lo), z: 4, core: 2. Of those that a mesh axis runs over, the one named last changes fastest.
Arguments:
- state: float32 [128, 768, 1104], P('lat', 'lon'), may hold values from -6 to 6
- background: float32 [128, 768, 1104], P('lat', 'lon'), may hold values from -6 to 6
- inv_background: float32 [1104], replicated, may hold values from 0.1 to 1
- w_embed: bfloat16 [1104, 256], replicated, may hold values from -0.1875 to 0.1875
- norm_gain: float32 [2, 2, 256], replicated, may hold values from 0.25 to 1.75
- w_qkv: bfloat16 [2, 256, 768], replicated, may hold values from -0.375 to 0.375
- w_proj: bfloat16 [2, 256, 256], replicated, may hold values from -0.375 to 0.375
- head_scale: float32 [2, 8], replicated, may hold values from 2 to 12
- w_up: bfloat16 [2, 256, 1024], replicated, may hold values from -0.375 to 0.375
- w_down: bfloat16 [2, 1024, 256], replicated, may hold values from -0.1875 to 0.1875
- w_head: bfloat16 [256, 1104], replicated, may hold values from -0.375 to 0.375
- w_obs1: float32 [69, 256], replicated, may hold values from -0.75 to 0.75
- w_obs2: float32 [256, 256], replicated, may hold values from -0.375 to 0.375
- r_inverse: float32 [256, 256], replicated, as said below
- obs_values: float32 [262144, 256], P(('lat', 'lon')), may hold values from -6 to 6
- obs_owner: int32 [262144, 1], P(('lat', 'lon')), may hold values from 0 to 127; in each aligned block of 2048 rows (0 to 2047, 2048 to 4095, ...) at most 32 rows name the same one
- obs_point: int32 [262144], P(('lat', 'lon')), may hold values from 0 to 12287
- obs_count: int32 [128], P(('lat', 'lon')), may hold values from 1024 to 2048, as said below
Outputs:
- gradient: float32 [128, 768, 1104], P('lat', 'lon')
The draws below stay inside these ranges and needn't reach their ends.
Inputs may be any that keep to these rules, and one draw needn't show every extreme that they name: `r_inverse`: Symmetric, with a positive diagonal larger than the sum of magnitudes of the rest of its row. `obs_owner`: among the slots of one device, at most 32 name the same owner, and in some device exactly 32 do. `obs_count`: some device has all its slots live.
All inputs are finite; a program needn't handle non-finite values.
Results may differ from the reference program's by a relative error of at most 0.018.
Values may be sent and summed in bfloat16 or wider, within the bound.
A program may use at most 192 MiB of HBM per device.

```python
import math
import jax
import jax.numpy as jnp
import numpy as np
from jax import lax

D = 256
HEADS = 8
FFN = 1024
VARS = 69
PIX = 16
CHAN = 256
HID_OBS = 256
WIN = 8
TLAT = 16
TLON = 48
OBS_DEV = 2048
SHIFT = 4
PV = 1104
NLAT = 128
NLON = 768
POINTS = 12288
OBS = 262144
CAP = 32
N_LAT = 8
N_LON = 16
DEVICES = 128


def draw_r_inverse(key, part):
    first, second = jax.random.split(jax.random.fold_in(key, 11))
    raw = 0.002 * jax.random.normal(first, (CHAN, CHAN), jnp.float32)
    sym = 0.5 * (raw + raw.T)
    extra = jnp.exp(jax.random.uniform(second, (CHAN,), jnp.float32, jnp.log(0.1), jnp.log(0.4)))
    off_part = sym - jnp.diag(jnp.diag(sym))
    return off_part + jnp.diag(jnp.sum(jnp.abs(off_part), 1) + extra)


def draw_obs_count(key, part):
    first, second = jax.random.split(jax.random.fold_in(key, 23))
    counts = jax.random.randint(first, (DEVICES,), OBS_DEV // 2, OBS_DEV + 1)
    chosen = jax.random.randint(second, (), 0, DEVICES)
    return jnp.where(jnp.arange(DEVICES) == chosen, OBS_DEV, counts).astype(jnp.int32)


def set_ends(values, key, smallest, top_value):
    shape = values.shape
    spot = [jax.random.randint(jax.random.fold_in(key, axis), (), 0, shape[axis]) for axis in range(len(shape))]
    values = values.at[tuple(spot)].set(smallest)
    longest = shape.index(max(shape))
    spot[longest] = (spot[longest] + 1) % shape[longest]
    return values.at[tuple(spot)].set(top_value)


def levels(stream_key, extent, cuts, smallest, top_value):
    def one(dim, shards_of):
        steps = jax.random.uniform(jax.random.fold_in(jax.random.fold_in(stream_key, 6), dim), (shards_of,), jnp.float32, smallest / len(cuts), top_value / len(cuts))
        return jnp.repeat(jnp.exp(steps), extent[dim] // shards_of).reshape((-1,) + (1,) * (len(extent) - dim - 1))

    loudness = one(*cuts[0])
    for cut in cuts[1:]:
        loudness = loudness * one(*cut)
    return loudness


def routed_block(key, own, number, rows, count, top, reach, slope):
    sequence = jax.random.permutation(key, count)
    packed, ordinary = shares(count, rows * top, reach, slope, True), shares(count, rows * top, reach, slope, False)
    places = jnp.arange(count)

    def named(tallies, rotation):
        used = int((tallies > 0).sum())
        fixed = max(1, used // 4)
        moved = fixed + (places - fixed + rotation * (used - fixed)) % max(1, count - fixed)
        return jnp.zeros((count,), jnp.int32).at[sequence[jnp.where(places < fixed, places, moved)]].set(jnp.asarray(tallies, jnp.int32))

    tallies = jnp.where(number % 4 == 0, named(packed, number // 4), named(ordinary, number - number // 4 - 1))
    mixed = jax.random.permutation(jax.random.fold_in(own, 3), count)
    donor, taker = mixed[0:count // 2 * 2:2], mixed[1:count // 2 * 2:2]
    room = jnp.minimum(tallies[donor] - 1, reach - tallies[taker]) // 2
    room = jnp.where((donor == sequence[0]) | (taker == sequence[0]) | (tallies[taker] == 0), 0, jnp.maximum(room, 0))
    moved = jax.random.randint(jax.random.fold_in(own, 4), (count // 2,), 0, 1 << 20) % (room + 1)
    tallies = tallies.at[donor].add(-moved).at[taker].add(moved)
    labels = jnp.searchsorted(jnp.cumsum(tallies), jnp.arange(rows * top), side="right").astype(jnp.int32)
    table = labels.reshape(top, rows).T
    table = table[jax.random.permutation(jax.random.fold_in(own, 1), rows)]
    rotation = jax.random.randint(jax.random.fold_in(own, 2), (rows, 1), 0, top)
    return jnp.take_along_axis(table, (jnp.arange(top)[None, :] + rotation) % top, axis=1)


def shares(amount, total, bound, lean, full):
    weights = [(1 << 20) // math.isqrt(standing ** lean) + 1 for standing in range(1, amount + 1)]
    largest = bound if full else min(bound, max(-(-total // amount), total * weights[0] // sum(weights)))
    least = 1 if total - largest >= amount - 1 else 0
    holding, rest = [largest] + [least] * (amount - 1), total - largest - least * (amount - 1)
    while rest > 0:
        movable = [i for i in range(1, amount) if holding[i] < largest] or [i for i in range(1, amount) if holding[i] < bound]
        pool, remaining = sum([weights[i] for i in movable]), rest
        for i in movable:
            more = min(bound - holding[i], max(1, remaining * weights[i] // pool), rest)
            holding[i] = holding[i] + more
            rest = rest - more
    return np.array(holding)


def bell_draw(stream_key, extent, scale, limit, cuts=(), held_as=jnp.bfloat16):
    values = scale * jax.random.normal(stream_key, extent, jnp.float32)
    if cuts:
        values = values * levels(stream_key, extent, cuts, -0.22, 0.18)
    return jnp.clip(values, -limit, limit).astype(held_as)


def setup_inputs(seed: int = 0) -> dict:
    seeds = jax.random.split(jax.random.key(seed), 19)
    state = bell_draw(seeds[0], (NLAT, NLON, PV), 1.0, 6.0, ((0, 8), (1, 16)), jnp.float32)
    background = bell_draw(seeds[1], (NLAT, NLON, PV), 1.0, 6.0, ((0, 8), (1, 16)), jnp.float32)
    inv_background = jnp.clip(jnp.exp(jax.random.uniform(seeds[2], (PV,), jnp.float32, math.log(0.1), math.log(1.0))), 0.1, 1.0)
    w_embed = bell_draw(seeds[3], (PV, D), PV ** -0.5, 0.1875)
    norm_gain = jnp.clip(1.0 + 0.15 * jax.random.normal(seeds[4], (2, 2, D), jnp.float32), 0.25, 1.75)
    w_qkv = bell_draw(seeds[5], (2, D, 3 * D), D ** -0.5, 0.375)
    w_proj = bell_draw(seeds[6], (2, D, D), D ** -0.5, 0.375)
    head_scale = jnp.clip(jnp.exp(jax.random.uniform(seeds[7], (2, HEADS), jnp.float32, math.log(2.0), math.log(12.0))), 2.0, 12.0)
    w_up = bell_draw(seeds[8], (2, D, FFN), D ** -0.5, 0.375)
    w_down = bell_draw(seeds[9], (2, FFN, D), FFN ** -0.5, 0.1875)
    w_head = bell_draw(seeds[10], (D, PV), D ** -0.5, 0.375)
    w_obs1 = bell_draw(seeds[11], (VARS, HID_OBS), VARS ** -0.5, 0.75, (), jnp.float32)
    w_obs2 = bell_draw(seeds[12], (HID_OBS, CHAN), HID_OBS ** -0.5, 0.375, (), jnp.float32)
    r_inverse = draw_r_inverse(jax.random.fold_in(seeds[18], 71), 0)
    obs_values = bell_draw(seeds[14], (OBS, CHAN), 1.0, 6.0, ((0, 128),), jnp.float32)
    obs_owner_keys = jax.random.split(jax.random.fold_in(seeds[15], 1), OBS // OBS_DEV)
    obs_owner_turns = jax.random.permutation(jax.random.fold_in(seeds[15], 3), OBS // OBS_DEV)
    obs_owner = jax.vmap(lambda own, number: routed_block(jax.random.fold_in(seeds[15], 2), own, number, OBS_DEV, DEVICES, 1, CAP, 2))(obs_owner_keys, obs_owner_turns).reshape((OBS, 1))
    obs_point = set_ends(jax.random.randint(seeds[16], (OBS,), 0, POINTS), jax.random.fold_in(seeds[16], 1), 0, POINTS - 1).astype(jnp.int32)
    obs_count = draw_obs_count(jax.random.fold_in(seeds[18], 71), 0)
    return {"state": state, "background": background, "inv_background": inv_background, "w_embed": w_embed, "norm_gain": norm_gain, "w_qkv": w_qkv, "w_proj": w_proj, "head_scale": head_scale, "w_up": w_up, "w_down": w_down, "w_head": w_head, "w_obs1": w_obs1, "w_obs2": w_obs2, "r_inverse": r_inverse, "obs_values": obs_values, "obs_owner": obs_owner, "obs_point": obs_point, "obs_count": obs_count}


EPS = 1e-05

def layer_norm(hidden, gain):
    mean = lax.optimization_barrier(jnp.mean(hidden, -1, keepdims=True))
    centred = hidden - mean
    spread = lax.optimization_barrier(jnp.mean(centred * centred, -1, keepdims=True))
    return (centred * lax.rsqrt(spread + EPS) * gain).astype(jnp.bfloat16)

def windows(field, width_win):
    rows, cols, width = field.shape
    field = field.reshape(rows // width_win, width_win, cols // width_win, width_win, width)
    return field.transpose(0, 2, 1, 3, 4).reshape(-1, width_win * width_win, width)

def unwindows(field, rows, cols, width_win):
    width = field.shape[-1]
    field = field.reshape(rows // width_win, cols // width_win, width_win, width_win, width)
    return field.transpose(0, 2, 1, 3, 4).reshape(rows, cols, width)

def attention(normed, w_qkv, w_proj, scales, row_start, total_rows, offset):
    rows, cols, width = normed.shape
    size = width // HEADS
    qkv = jnp.dot(normed.reshape(-1, width), w_qkv, preferred_element_type=jnp.float32).astype(jnp.bfloat16)
    qkv = windows(qkv.reshape(rows, cols, 3 * width), WIN)
    count = qkv.shape[0]
    query = qkv[:, :, :width].reshape(count, WIN * WIN, HEADS, size).astype(jnp.float32)
    keys = qkv[:, :, width:2 * width].reshape(count, WIN * WIN, HEADS, size).astype(jnp.float32)
    values = qkv[:, :, 2 * width:].reshape(count, WIN * WIN, HEADS, size).astype(jnp.float32)
    query = (query * lax.rsqrt(lax.optimization_barrier(jnp.sum(query * query, -1, keepdims=True)) + 1.0)).astype(jnp.bfloat16)
    keys = (keys * lax.rsqrt(lax.optimization_barrier(jnp.sum(keys * keys, -1, keepdims=True)) + 1.0)).astype(jnp.bfloat16)
    scores = jnp.einsum('wqhd,wkhd->whqk', query.astype(jnp.float32), keys.astype(jnp.float32))
    scores = scores * scales[None, :, None, None]
    expo = jnp.exp(scores)
    if offset > 0:
        row_index = row_start + jnp.arange(rows, dtype=jnp.int32)
        side = (row_index >= total_rows - offset).astype(jnp.float32)
        side = windows(jnp.broadcast_to(side[:, None, None], (rows, cols, 1)), WIN)[:, :, 0]
        allowed = (side[:, :, None] == side[:, None, :]).astype(jnp.float32)
        expo = expo * allowed[:, None, :, :]
    probs = (expo / lax.optimization_barrier(jnp.sum(expo, -1, keepdims=True))).astype(jnp.bfloat16)
    mixed = jnp.einsum('whqk,wkhd->wqhd', probs.astype(jnp.float32), values).astype(jnp.bfloat16)
    mixed = unwindows(mixed.reshape(count, WIN * WIN, width), rows, cols, WIN)
    out = jnp.dot(mixed.reshape(-1, width), w_proj, preferred_element_type=jnp.float32)
    return out.astype(jnp.bfloat16).reshape(rows, cols, width)

def mlp_residual(hidden, gain, w_up, w_down):
    width = hidden.shape[-1]
    normed = layer_norm(hidden, gain).reshape(-1, width)
    inner = jax.nn.gelu(jnp.dot(normed, w_up, preferred_element_type=jnp.float32)).astype(jnp.bfloat16)
    return hidden + jnp.dot(inner, w_down, preferred_element_type=jnp.float32).reshape(hidden.shape)

def propagate(state, w_embed, norm_gain, w_qkv, w_proj, head_scale, w_up, w_down, w_head):
    rows, cols, values = state.shape
    hidden = jnp.dot(state.astype(jnp.bfloat16).reshape(-1, values), w_embed, preferred_element_type=jnp.float32)
    hidden = hidden.reshape(rows, cols, -1)
    hidden = hidden + attention(layer_norm(hidden, norm_gain[0, 0]), w_qkv[0], w_proj[0], head_scale[0], 0, rows, 0)
    hidden = mlp_residual(hidden, norm_gain[0, 1], w_up[0], w_down[0])
    normed = layer_norm(hidden, norm_gain[1, 0])
    rolled = jnp.roll(normed, (-SHIFT, -SHIFT), (0, 1))
    answer = attention(rolled, w_qkv[1], w_proj[1], head_scale[1], 0, rows, SHIFT)
    hidden = hidden + jnp.roll(answer, (SHIFT, SHIFT), (0, 1))
    hidden = mlp_residual(hidden, norm_gain[1, 1], w_up[1], w_down[1])
    lifted = jnp.dot(hidden.astype(jnp.bfloat16).reshape(rows * cols, -1), w_head, preferred_element_type=jnp.float32)
    return state + lifted.reshape(state.shape)

def radiance_cost(columns, observed, live, w_obs1, w_obs2, r_inverse):
    best = lax.Precision.HIGHEST
    inner = jnp.tanh(jnp.dot(columns, w_obs1, precision=best))
    innovation = (jnp.dot(inner, w_obs2, precision=best) - observed) * live[:, None]
    return 0.5 * jnp.sum(innovation * jnp.dot(innovation, r_inverse, precision=best))

def reference(state, background, inv_background, w_embed, norm_gain, w_qkv, w_proj, head_scale, w_up, w_down, w_head, w_obs1, w_obs2, r_inverse, obs_values, obs_owner, obs_point, obs_count):

    def cost(initial):
        moved = propagate(initial, w_embed, norm_gain, w_qkv, w_proj, head_scale, w_up, w_down, w_head)
        grid = moved.reshape(N_LAT, TLAT, N_LON, TLON, PIX, VARS).transpose(0, 2, 1, 3, 4, 5)
        grid = grid.reshape(N_LAT * N_LON, TLAT * TLON * PIX, VARS)
        columns = grid[obs_owner[:, 0].astype(jnp.int32), obs_point.astype(jnp.int32)]
        slot_index = jnp.arange(OBS_DEV * N_LAT * N_LON, dtype=jnp.int32) % OBS_DEV
        live = (slot_index < jnp.repeat(obs_count, OBS_DEV)).astype(jnp.float32)
        differ = initial - background
        prior = 0.5 * jnp.sum(inv_background * differ * differ)
        return prior + radiance_cost(columns, obs_values, live, w_obs1, w_obs2, r_inverse)
    value, pull = jax.vjp(cost, state)
    return pull(jnp.ones_like(value))[0]
```

```python
import functools

import jax
import jax.numpy as jnp
import numpy as np
from jax import lax
from jax.experimental import pallas as pl
from jax.experimental.pallas import tpu as pltpu
from jax.sharding import PartitionSpec as P

F32 = jnp.float32
BF16 = jnp.bfloat16
EPS = 1e-05
VARS = 69
PIX = 16
HEADS = 8
D = 256
FFN = 1024
PV = 1104
T = 768
BLK = 16
WT = 64
BR, BC = 4, 12
SW_R, SW_C = 3, 7
TX = SW_R * SW_C * WT
CAP = 32
DEV = 128
SLOTS = DEV * CAP
OBS = 2048
CHAN = 256
WIDE = 384
VMEM = pl.BlockSpec(memory_space=pltpu.VMEM)
SMEM = pl.BlockSpec(memory_space=pltpu.SMEM)


def mm(a, b):
    return jnp.dot(a, b, preferred_element_type=F32)


def mm_nt(a, b):
    return lax.dot_general(a, b, (((1,), (1,)), ((), ())), preferred_element_type=F32)


def mm_tn(a, b):
    return lax.dot_general(a, b, (((0,), (0,)), ((), ())), preferred_element_type=F32)


def call(kernel, outs, scratch=(), limit=48, **kw):
    params = {k: kw.pop(k) for k in ("collective_id", "has_side_effects") if k in kw}
    return pl.pallas_call(
        kernel,
        out_shape=[jax.ShapeDtypeStruct(s, d) for s, d in outs],
        out_specs=[VMEM] * len(outs),
        scratch_shapes=list(scratch),
        compiler_params=pltpu.CompilerParams(vmem_limit_bytes=limit << 20, **params),
        **kw,
    )


def block_at(bi, bj):
    return (((bi // 2) * (BC // 2) + bj // 2) * 4 + (bi % 2) * 2 + bj % 2) * BLK


def row_of_place():
    out = np.zeros((T,), np.int32)
    for bi in range(BR):
        for bj in range(BC):
            for k in range(BLK):
                out[block_at(bi, bj) + k] = (bi * 4 + k // 4) * (BC * 4) + bj * 4 + k % 4
    return out


ORDER = row_of_place()
PLACE = np.argsort(ORDER).astype(np.int32)


def permutation(column_ref):
    return (lax.broadcasted_iota(jnp.int32, (T, T), 1) == column_ref[...]).astype(BF16)


def norm_parts(x):
    centred = x - jnp.mean(x, -1, keepdims=True)
    scale = lax.rsqrt(jnp.mean(centred * centred, -1, keepdims=True) + EPS)
    return centred * scale, scale


def norm(x, gain):
    return (norm_parts(x)[0] * gain).astype(BF16)


def norm_back(x, gain, dy):
    unit, scale = norm_parts(x)
    dn = dy * gain
    return scale * (dn - jnp.mean(dn, -1, keepdims=True) - unit * jnp.mean(dn * unit, -1, keepdims=True))


def same_group(n, size):
    a = lax.broadcasted_iota(jnp.int32, (n, n), 0) // size
    b = lax.broadcasted_iota(jnp.int32, (n, n), 1) // size
    return (a == b).astype(BF16)


def head_mask():
    a = lax.broadcasted_iota(jnp.int32, (HEADS * WT, D), 0) // WT
    b = lax.broadcasted_iota(jnp.int32, (HEADS * WT, D), 1) // (D // HEADS)
    return (a == b).astype(BF16)


def unit_scale(q, ones32):
    return lax.rsqrt(mm((q * q).astype(BF16), ones32) + 1.0)


def spread(x, hmask):
    return jnp.concatenate([x] * HEADS, 0) * hmask


def gather_heads(x, hmask):
    x = x * hmask.astype(F32)
    out = x[:WT]
    for h in range(1, HEADS):
        out = out + x[h * WT : (h + 1) * WT]
    return out


def attend(count, qkv_ref, p_ref, scale, factor, put):
    ones32 = same_group(D, D // HEADS)
    ones64 = same_group(HEADS * WT, WT)
    hmask = head_mask()
    for w in range(count):
        rows = pl.ds(w * WT, WT)
        q = qkv_ref[rows, :D].astype(F32)
        k = qkv_ref[rows, D : 2 * D].astype(F32)
        v = qkv_ref[rows, 2 * D :]
        qn = (q * unit_scale(q, ones32)).astype(BF16)
        kn = (k * unit_scale(k, ones32)).astype(BF16)
        e = jnp.exp(mm_nt(qn, spread(kn, hmask)) * scale)
        f = factor(w)
        if f is not None:
            e = e * f
        p = (e / mm(e.astype(BF16), ones64)).astype(BF16)
        p_ref[rows, :] = p
        put(w, mm(p, spread(v, hmask)).astype(BF16))


def attend_back(count, qkv_ref, p_ref, scale, take, put):
    ones32 = same_group(D, D // HEADS)
    ones64 = same_group(HEADS * WT, WT)
    hmask = head_mask()

    def through_unit(x, r, dn):
        inner = mm((x * dn).astype(BF16), ones32)
        return (r * dn - x * (r * r * r) * inner).astype(BF16)

    for w in range(count):
        rows = pl.ds(w * WT, WT)
        q = qkv_ref[rows, :D].astype(F32)
        k = qkv_ref[rows, D : 2 * D].astype(F32)
        v = qkv_ref[rows, 2 * D :]
        rq = unit_scale(q, ones32)
        rk = unit_scale(k, ones32)
        qn = (q * rq).astype(BF16)
        kbd = spread((k * rk).astype(BF16), hmask)
        do = take(w)
        p = p_ref[rows, :]
        dp = mm_nt(do, spread(v, hmask))
        pd = p.astype(F32) * dp
        ds = pd - p.astype(F32) * mm(pd.astype(BF16), ones64)
        ds = (ds * scale).astype(BF16)
        dqn = mm(ds, kbd)
        dkn = gather_heads(mm_tn(ds, qn), hmask)
        dv = gather_heads(mm_tn(p, do), hmask).astype(BF16)
        put(w, through_unit(q, rq, dqn), through_unit(k, rk, dkn), dv)


ROWS = 256


def feed(hm_ref, gain, wup_ref, wdown_ref, gp_ref, put):
    for i in range(T // ROWS):
        rows = pl.ds(i * ROWS, ROWS)
        h = hm_ref[rows, :]
        u = mm(norm(h, gain), wup_ref[...])
        c = 0.7978845608028654
        square = u * u
        t = jnp.tanh(u * (c + (c * 0.044715) * square))
        half = 0.5 + 0.5 * t
        gp_ref[rows, :] = (half + 0.5 * u * (1.0 - t * t) * (c + (3.0 * c * 0.044715) * square)).astype(BF16)
        put(rows, h + mm((u * half).astype(BF16), wdown_ref[...]))


def feed_back(rows, dh, hm_ref, gain, wup_ref, wdown_ref, gp_ref):
    dg = mm_nt(dh.astype(BF16), wdown_ref[...])
    du = (dg * gp_ref[rows, :].astype(F32)).astype(BF16)
    dn = mm_nt(du, wup_ref[...])
    return dh + norm_back(hm_ref[rows, :], gain, dn)


def route_kernel(owner_ref, count_ref, values_ref, aux_ref, out_ref, target_ref, wide_ref):
    step = 256
    upper = (
        lax.broadcasted_iota(jnp.int32, (step, step), 0) < lax.broadcasted_iota(jnp.int32, (step, step), 1)
    ).astype(BF16)
    carry = jnp.zeros((DEV, 1), F32)
    for i in range(OBS // step):
        owner = owner_ref[:, i * step : (i + 1) * step]
        live = (lax.broadcasted_iota(jnp.int32, (1, step), 1) + i * step) < count_ref[0]
        owner = jnp.where(live, owner, -1)
        hot = (lax.broadcasted_iota(jnp.int32, (DEV, step), 0) == owner).astype(F32)
        before = mm(hot.astype(BF16), upper) + carry
        carry = carry + jnp.sum(hot, 1, keepdims=True)
        place = jnp.sum(before * hot, 0, keepdims=True).astype(jnp.int32)
        target_ref[:, i * step : (i + 1) * step] = jnp.where(live, owner * CAP + place, -1)
    wide_ref[:, :CHAN] = values_ref[...].astype(BF16)
    wide_ref[:, CHAN:] = aux_ref[...]
    target = target_ref[...]
    row = lax.broadcasted_iota(jnp.int32, (step, OBS), 0)
    for i in range(SLOTS // step):
        pick = (row == target - i * step).astype(BF16)
        out_ref[pl.ds(i * step, step), :] = mm(pick, wide_ref[...]).astype(BF16)


def route(owner, point, count, values):
    patch = point // PIX
    lane = jnp.arange(DEV, dtype=jnp.int32)[None, :]
    place = jnp.where(lane == 0, (patch // PIX)[:, None], (patch % PIX)[:, None])
    place = jnp.where(lane == 2, (point % PIX)[:, None], place)
    place = jnp.where(lane == 3, 1, place)
    aux = jnp.where(lane < 4, place, 0).astype(BF16)
    return call(
        route_kernel,
        [((SLOTS, WIDE), BF16)],
        [pltpu.VMEM((1, OBS), jnp.int32), pltpu.VMEM((OBS, WIDE), BF16)],
        in_specs=[VMEM, SMEM, VMEM, VMEM],
    )(owner.reshape(1, OBS), count, values, aux)[0]


def first_kernel(
    state_ref, order_ref, wemb_ref, gain_ref, wqkv_ref, wproj_ref, scale_ref, wup_ref, wdown_ref,
    h0_ref, hm_ref, h1_ref, z1_ref, qkv_ref, p_ref, gp_ref, o_ref, sb_ref,
):
    sb_ref[...] = state_ref[...].astype(BF16)
    perm = permutation(order_ref)
    for i in range(T // ROWS):
        rows = pl.ds(i * ROWS, ROWS)
        mine = mm(perm[i * ROWS : (i + 1) * ROWS], sb_ref[...]).astype(BF16)
        h0 = mm(mine, wemb_ref[...])
        h0_ref[rows, :] = h0
        qkv_ref[rows, :] = mm(norm(h0, gain_ref[0, 0:1, :]), wqkv_ref[...]).astype(BF16)

    def put(w, o):
        o_ref[pl.ds(w * WT, WT), :] = o

    attend(T // WT, qkv_ref, p_ref, scale_ref[...], lambda w: None, put)
    hm_ref[...] = h0_ref[...] + mm(o_ref[...], wproj_ref[...]).astype(BF16).astype(F32)

    def put_out(rows, h1):
        h1_ref[rows, :] = h1
        z1_ref[rows, :] = norm(h1, gain_ref[1, 0:1, :])

    feed(hm_ref, gain_ref[0, 1:2, :], wup_ref, wdown_ref, gp_ref, put_out)


SIDES = [(-1, 0), (1, 0), (0, -1), (0, 1), (-1, -1), (-1, 1), (1, -1), (1, 1)]
SHAPES = [(6, 2), (6, 2), (2, 2), (2, 2), (), (), (), ()]
PACKED = (2, 6, 2, 2, BLK, D)


def edge(ref, side):
    r, c = side
    i, j = (0 if r < 0 else 1), (0 if c < 0 else 1)
    if c == 0:
        return ref.at[i, :, i]
    if r == 0:
        return ref.at[:, 5 * j, :, j]
    return ref.at[i, 5 * j, i, j]


def exchange_kernel(n_lat, n_lon, z_ref, *refs):
    halos, send, recv = refs[:8], refs[8], refs[9]
    lat, lon = lax.axis_index("lat"), lax.axis_index("lon")

    def at(side):
        return (lax.rem(lat + side[0] + n_lat, n_lat), lax.rem(lon + side[1] + n_lon, n_lon))

    barrier = pltpu.get_barrier_semaphore()
    for side in SIDES:
        pl.semaphore_signal(barrier, inc=1, device_id=at(side), device_id_type=pl.DeviceIdType.MESH)
    pl.semaphore_wait(barrier, 8)
    copies = []
    for n, side in enumerate(SIDES):
        opposite = SIDES.index((-side[0], -side[1]))
        copies.append(
            pltpu.make_async_remote_copy(
                src_ref=edge(z_ref, side),
                dst_ref=halos[opposite],
                send_sem=send.at[n],
                recv_sem=recv.at[opposite],
                device_id=at(side),
                device_id_type=pl.DeviceIdType.MESH,
            )
        )
        copies[-1].start()
    for copy in copies:
        copy.wait()


def exchange(z, n_lat, n_lon, number):
    return call(
        functools.partial(exchange_kernel, n_lat, n_lon),
        [(s + (BLK, D), BF16) for s in SHAPES],
        [pltpu.SemaphoreType.DMA((8,)), pltpu.SemaphoreType.DMA((8,))],
        limit=8,
        in_specs=[VMEM],
        collective_id=number,
        has_side_effects=True,
    )(z.reshape(PACKED))


def shifted_blocks():
    for si in range(SW_R):
        for sj in range(SW_C):
            for k in range(4):
                yield ((si * SW_C + sj) * 4 + k) * BLK, 2 * si - 1 + k // 2, 2 * sj - 1 + k % 2


def inside(bi, bj):
    return 0 <= bi < BR and 0 <= bj < BC


def fill_shifted(out_ref, z_ref, halos):
    for row, bi, bj in shifted_blocks():
        if inside(bi, bj):
            out_ref[pl.ds(row, BLK), :] = z_ref[pl.ds(block_at(bi, bj), BLK), :]
            continue
        r = -1 if bi < 0 else 1 if bi >= BR else 0
        c = -1 if bj < 0 else 1 if bj >= BC else 0
        halo = halos[SIDES.index((r, c))]
        if c == 0:
            value = halo[bj // 2, bj % 2]
        elif r == 0:
            value = halo[bi // 2, bi % 2]
        else:
            value = halo[...]
        out_ref[pl.ds(row, BLK), :] = value


def second_kernel(
    flag_ref, h1_ref, z1_ref, a0, a1, a2, a3, a4, a5, a6, a7, state_ref, place_ref, gain_ref, wqkv_ref,
    wproj_ref, scale_ref, wup_ref, wdown_ref, whead_ref,
    hm_ref, qkv_ref, p_ref, gp_ref, moved_ref, zs_ref, o_ref, h3_ref,
):
    fill_shifted(zs_ref, z1_ref, (a0, a1, a2, a3, a4, a5, a6, a7))
    step = TX // 3
    for i in range(3):
        rows = pl.ds(i * step, step)
        qkv_ref[rows, :] = mm(zs_ref[rows, :], wqkv_ref[...]).astype(BF16)
    a = lax.broadcasted_iota(jnp.int32, (WT, HEADS * WT), 0) // (2 * BLK)
    b = lax.broadcasted_iota(jnp.int32, (WT, HEADS * WT), 1) // (2 * BLK) % 2
    apart = (a != b).astype(F32)
    top = 1.0 - apart * flag_ref[0].astype(F32)
    bottom = 1.0 - apart * flag_ref[1].astype(F32)

    def factor(w):
        return {0: top, SW_R - 1: bottom}.get(w // SW_C)

    def put(w, o):
        for row, bi, bj in shifted_blocks():
            if row // WT == w and inside(bi, bj):
                o_ref[pl.ds(block_at(bi, bj), BLK), :] = o[row % WT : row % WT + BLK]

    attend(SW_R * SW_C, qkv_ref, p_ref, scale_ref[...], factor, put)
    hm_ref[...] = h1_ref[...] + mm(o_ref[...], wproj_ref[...]).astype(BF16).astype(F32)

    def put_out(rows, h3):
        h3_ref[rows, :] = h3.astype(BF16)

    feed(hm_ref, gain_ref[1, 1:2, :], wup_ref, wdown_ref, gp_ref, put_out)
    perm = permutation(place_ref)
    for i in range(T // ROWS):
        rows = pl.ds(i * ROWS, ROWS)
        mine = mm(perm[i * ROWS : (i + 1) * ROWS], h3_ref[...]).astype(BF16)
        moved_ref[rows, :] = (state_ref[rows, :] + mm(mine, whead_ref[...])).astype(BF16)


def radiance_kernel(
    recv_ref, moved_ref, pixel_ref, w1_ref, w2_ref, rinv_ref, gm_ref, hot_ref, adj_ref,
):
    step = 256
    pick = (
        lax.broadcasted_iota(jnp.int32, (8, DEV), 0) == lax.broadcasted_iota(jnp.int32, (8, DEV), 1)
    ).astype(BF16)
    lane = lax.broadcasted_iota(jnp.int32, (step, T), 1)
    row = lax.broadcasted_iota(jnp.int32, (T, step), 0)
    w2 = w2_ref[...].astype(BF16)
    rinv = rinv_ref[...].astype(BF16)
    pixel = pixel_ref[...]

    def chunk(i, _):
        rows = pl.ds(pl.multiple_of(i * step, step), step)
        aux16 = recv_ref[rows, CHAN:]
        aux = aux16.astype(F32)
        live = aux[:, 3:4]
        patch = jnp.where(live > 0, aux[:, 0:1] * PIX + aux[:, 1:2], -1.0).astype(jnp.int32)
        hot = (lane == patch).astype(BF16)
        flat = mm_nt(pick, aux16)
        across = jnp.where(flat[3:4] > 0, flat[0:1] * PIX + flat[1:2], -1.0).astype(jnp.int32)
        hot_ref[:, rows] = (row == across).astype(BF16)
        here = pixel == aux[:, 2:3]
        found = jnp.where(here, mm(hot, moved_ref[...]), 0.0).astype(BF16)
        inner = jnp.tanh(mm(found, w1_ref[...]))
        innovation = (mm(inner.astype(BF16), w2) - recv_ref[rows, :CHAN].astype(F32)) * live
        weighted = mm(innovation.astype(BF16), rinv).astype(BF16)
        pulled = mm_nt(weighted, w2) * (1.0 - inner * inner)
        adj_ref[rows, :] = jnp.where(here, mm_nt(pulled.astype(BF16), w1_ref[...]), 0.0).astype(BF16)
        return 0

    lax.fori_loop(0, SLOTS // step, chunk, 0)
    for i in range(T // ROWS):
        rows = pl.ds(i * ROWS, ROWS)
        gm_ref[rows, :] = mm(hot_ref[rows, :], adj_ref[...])


def back_head_kernel(gm_ref, order_ref, whead_ref, hm_ref, gain_ref, wup_ref, wdown_ref, gp_ref, dh_ref, da_ref, d3_ref):
    for i in range(T // ROWS):
        rows = pl.ds(i * ROWS, ROWS)
        d3_ref[rows, :] = mm_nt(gm_ref[rows, :].astype(BF16), whead_ref[...]).astype(BF16)
    perm = permutation(order_ref)
    for i in range(T // ROWS):
        rows = pl.ds(i * ROWS, ROWS)
        d3 = mm(perm[i * ROWS : (i + 1) * ROWS], d3_ref[...])
        d2 = feed_back(rows, d3, hm_ref, gain_ref[1, 1:2, :], wup_ref, wdown_ref, gp_ref)
        dh_ref[rows, :] = d2
        da_ref[rows, :] = d2.astype(BF16)


def back_kernel(
    dh2_ref, da_ref, a0, a1, a2, a3, a4, a5, a6, a7, place_ref, gain_ref,
    wqkv1_ref, wproj1_ref, scale1_ref, qkv1_ref, p1_ref, h1_ref,
    wqkv0_ref, wproj0_ref, scale0_ref, qkv0_ref, p0_ref, hm0_ref, h0_ref, wup_ref, wdown_ref, gp_ref,
    out_ref, das_ref, do_ref, dqkv_ref, dh_ref, d0_ref,
):
    fill_shifted(das_ref, da_ref, (a0, a1, a2, a3, a4, a5, a6, a7))
    step = TX // 3
    for i in range(3):
        rows = pl.ds(i * step, step)
        do_ref[rows, :] = mm_nt(das_ref[rows, :], wproj1_ref[...]).astype(BF16)

    def take(w):
        return do_ref[pl.ds(w * WT, WT), :]

    def put_shifted(w, dq, dk, dv):
        for row, bi, bj in shifted_blocks():
            if row // WT == w and inside(bi, bj):
                mine, there = slice(row % WT, row % WT + BLK), pl.ds(block_at(bi, bj), BLK)
                dqkv_ref[there, :D] = dq[mine]
                dqkv_ref[there, D : 2 * D] = dk[mine]
                dqkv_ref[there, 2 * D :] = dv[mine]

    attend_back(SW_R * SW_C, qkv1_ref, p1_ref, scale1_ref[...], take, put_shifted)
    for i in range(T // ROWS):
        rows = pl.ds(i * ROWS, ROWS)
        dz = mm_nt(dqkv_ref[rows, :], wqkv1_ref[...])
        d1 = dh2_ref[rows, :] + norm_back(h1_ref[rows, :], gain_ref[1, 0:1, :], dz)
        dm = feed_back(rows, d1, hm0_ref, gain_ref[0, 1:2, :], wup_ref, wdown_ref, gp_ref)
        dh_ref[rows, :] = dm
        do_ref[rows, :] = mm_nt(dm.astype(BF16), wproj0_ref[...]).astype(BF16)

    def put(w, dq, dk, dv):
        there = pl.ds(w * WT, WT)
        dqkv_ref[there, :D] = dq
        dqkv_ref[there, D : 2 * D] = dk
        dqkv_ref[there, 2 * D :] = dv

    attend_back(T // WT, qkv0_ref, p0_ref, scale0_ref[...], take, put)
    for i in range(T // ROWS):
        rows = pl.ds(i * ROWS, ROWS)
        dz = mm_nt(dqkv_ref[rows, :], wqkv0_ref[...])
        d0_ref[rows, :] = (dh_ref[rows, :] + norm_back(h0_ref[rows, :], gain_ref[0, 0:1, :], dz)).astype(BF16)
    perm = permutation(place_ref)
    out_ref[...] = mm(perm, d0_ref[...]).astype(BF16)


def last_kernel(d0_ref, wemb_ref, gm_ref, state_ref, background_ref, inverse_ref, out_ref):
    prior = inverse_ref[...] * (state_ref[...] - background_ref[...])
    out_ref[...] = gm_ref[...] + mm_nt(d0_ref[...], wemb_ref[...]) + prior


def last(d0, w_embed, gm, state, background, inverse):
    step = 128
    part = pl.BlockSpec((step, PV), lambda i: (i, 0))
    return pl.pallas_call(
        last_kernel,
        grid=(T // step,),
        out_shape=jax.ShapeDtypeStruct((T, PV), F32),
        in_specs=[
            pl.BlockSpec((step, D), lambda i: (i, 0)),
            pl.BlockSpec((PV, D), lambda i: (0, 0)),
            part, part, part,
            pl.BlockSpec((1, PV), lambda i: (0, 0)),
        ],
        out_specs=part,
        compiler_params=pltpu.CompilerParams(vmem_limit_bytes=24 << 20),
    )(d0, w_embed, gm, state, background, inverse)


def local(
    n_lat, n_lon, state, background, inv_background, w_embed, norm_gain, w_qkv, w_proj, head_scale, w_up,
    w_down, w_head, w_obs1, w_obs2, r_inverse, obs_values, obs_owner, obs_point, obs_count,
):
    flat = state.reshape(T, PV)
    order = jnp.asarray(ORDER).reshape(T, 1)
    place = jnp.asarray(PLACE).reshape(T, 1)
    scales = jnp.repeat(head_scale, WT, axis=1)
    w1 = jnp.tile(w_obs1.astype(BF16), (PIX, 1))
    pixel = (jnp.arange(PV, dtype=jnp.int32) // VARS).astype(F32).reshape(1, PV)
    lat = lax.axis_index("lat")
    flags = jnp.stack([lat == 0, lat == n_lat - 1]).astype(jnp.int32)

    sent = route(obs_owner, obs_point, obs_count, obs_values)
    recv = lax.all_to_all(
        sent.reshape(DEV, CAP, WIDE), ("lat", "lon"), split_axis=0, concat_axis=0, tiled=True
    ).reshape(SLOTS, WIDE)

    h0, hm0, h1, z1, qkv0, p0, gp0 = call(
        first_kernel,
        [((T, D), F32)] * 3
        + [((T, D), BF16), ((T, 3 * D), BF16), ((T, HEADS * WT), BF16), ((T, FFN), BF16)],
        [pltpu.VMEM((T, D), BF16), pltpu.VMEM((T, PV), BF16)],
        in_specs=[VMEM] * 9,
    )(flat, order, w_embed, norm_gain, w_qkv[0], w_proj[0], scales[0:1], w_up[0], w_down[0])
    halo = exchange(z1, n_lat, n_lon, 1)
    hm1, qkv1, p1, gp1, moved = call(
        second_kernel,
        [((T, D), F32), ((TX, 3 * D), BF16), ((TX, HEADS * WT), BF16), ((T, FFN), BF16), ((T, PV), BF16)],
        [pltpu.VMEM((TX, D), BF16), pltpu.VMEM((T, D), BF16), pltpu.VMEM((T, D), BF16)],
        in_specs=[SMEM] + [VMEM] * 19,
    )(flags, h1, z1, *halo, flat, place, norm_gain, w_qkv[1], w_proj[1], scales[1:2], w_up[1], w_down[1], w_head)
    (gm,) = call(
        radiance_kernel,
        [((T, PV), F32)],
        [pltpu.VMEM((T, SLOTS), BF16), pltpu.VMEM((SLOTS, PV), BF16)],
        in_specs=[VMEM] * 6,
    )(recv, moved, pixel, w1, w_obs2, r_inverse)
    dh2, da = call(
        back_head_kernel,
        [((T, D), F32), ((T, D), BF16)],
        [pltpu.VMEM((T, D), BF16)],
        in_specs=[VMEM] * 8,
    )(gm, order, w_head, hm1, norm_gain, w_up[1], w_down[1], gp1)
    halo = exchange(da, n_lat, n_lon, 2)
    (d0,) = call(
        back_kernel,
        [((T, D), BF16)],
        [
            pltpu.VMEM((TX, D), BF16),
            pltpu.VMEM((TX, D), BF16),
            pltpu.VMEM((T, 3 * D), BF16),
            pltpu.VMEM((T, D), F32),
            pltpu.VMEM((T, D), BF16),
        ],
        in_specs=[VMEM] * 28,
    )(
        dh2, da, *halo, place, norm_gain,
        w_qkv[1], w_proj[1], scales[1:2], qkv1, p1, h1,
        w_qkv[0], w_proj[0], scales[0:1], qkv0, p0, hm0, h0, w_up[0], w_down[0], gp0,
    )
    out = last(d0, w_embed, gm, flat, background.reshape(T, PV), inv_background.reshape(1, PV))
    return out.reshape(state.shape)


def solution(mesh):
    grid = P("lat", "lon", None)
    slots = P(("lat", "lon"))
    placed = (grid, grid) + (P(),) * 12 + (P(("lat", "lon"), None),) * 2 + (slots, slots)
    return jax.shard_map(
        functools.partial(local, mesh.shape["lat"], mesh.shape["lon"]),
        mesh=mesh,
        in_specs=placed,
        out_specs=grid,
        check_vma=False,
    )
```

```python
import functools

import jax
import jax.numpy as jnp
import numpy as np
from jax import lax
from jax.experimental import pallas as pl
from jax.experimental.pallas import tpu as pltpu
from jax.sharding import PartitionSpec as P

F32 = jnp.float32
BF16 = jnp.bfloat16
EPS = 1e-05
VARS = 69
PIX = 16
HEADS = 8
D = 256
FFN = 1024
PV = 1104
T = 768
BLK = 16
WT = 64
BR, BC = 4, 12
SW_R, SW_C = 3, 7
TX = SW_R * SW_C * WT
CAP = 32
DEV = 128
SLOTS = DEV * CAP
OBS = 2048
CHAN = 256
WIDE = 384
VMEM = pl.BlockSpec(memory_space=pltpu.VMEM)
SMEM = pl.BlockSpec(memory_space=pltpu.SMEM)


def mm(a, b):
    return jnp.dot(a, b, preferred_element_type=F32)


def mm_nt(a, b):
    return lax.dot_general(a, b, (((1,), (1,)), ((), ())), preferred_element_type=F32)


def mm_tn(a, b):
    return lax.dot_general(a, b, (((0,), (0,)), ((), ())), preferred_element_type=F32)


def call(kernel, outs, scratch=(), limit=48, **kw):
    params = {k: kw.pop(k) for k in ("collective_id", "has_side_effects") if k in kw}
    return pl.pallas_call(
        kernel,
        out_shape=[jax.ShapeDtypeStruct(s, d) for s, d in outs],
        out_specs=[VMEM] * len(outs),
        scratch_shapes=list(scratch),
        compiler_params=pltpu.CompilerParams(vmem_limit_bytes=limit << 20, **params),
        **kw,
    )


def block_at(bi, bj):
    return (((bi // 2) * (BC // 2) + bj // 2) * 4 + (bi % 2) * 2 + bj % 2) * BLK


def row_of_place():
    out = np.zeros((T,), np.int32)
    for bi in range(BR):
        for bj in range(BC):
            for k in range(BLK):
                out[block_at(bi, bj) + k] = (bi * 4 + k // 4) * (BC * 4) + bj * 4 + k % 4
    return out


ORDER = row_of_place()
PLACE = np.argsort(ORDER).astype(np.int32)


def permutation(column):
    return (lax.broadcasted_iota(jnp.int32, (T, T), 1) == column).astype(BF16)


def norm_parts(x):
    centred = x - jnp.mean(x, -1, keepdims=True)
    scale = lax.rsqrt(jnp.mean(centred * centred, -1, keepdims=True) + EPS)
    return centred * scale, scale


def norm(x, gain):
    return (norm_parts(x)[0] * gain).astype(BF16)


def norm_back(x, gain, dy):
    unit, scale = norm_parts(x)
    dn = dy * gain
    return scale * (dn - jnp.mean(dn, -1, keepdims=True) - unit * jnp.mean(dn * unit, -1, keepdims=True))


def same_group(n, size):
    a = lax.broadcasted_iota(jnp.int32, (n, n), 0) // size
    b = lax.broadcasted_iota(jnp.int32, (n, n), 1) // size
    return (a == b).astype(BF16)


HALF = D // 2
GROUP = 4 * WT


def head_mask():
    a = lax.broadcasted_iota(jnp.int32, (GROUP, HALF), 0) // WT
    b = lax.broadcasted_iota(jnp.int32, (GROUP, HALF), 1) // (D // HEADS)
    return (a == b).astype(BF16)


def spread(x, hmask):
    return jnp.concatenate([x] * 4, 0) * hmask


def gather_heads(x):
    lane = lax.broadcasted_iota(jnp.int32, (WT, HALF), 1) // (D // HEADS)
    out = x[:WT]
    for h in range(1, 4):
        out = jnp.where(lane == h, x[h * WT : (h + 1) * WT], out)
    return out


def project(z, wqkv, ones32):
    qkv = mm(z, wqkv).astype(BF16)
    parts, factors = [], []
    for n in range(2):
        x = qkv[:, n * D : (n + 1) * D].astype(F32)
        r = lax.rsqrt(mm((x * x).astype(BF16), ones32) + 1.0)
        parts.append((x * r).astype(BF16))
        factors.append(r.astype(BF16))
    return jnp.concatenate(parts + [qkv[:, 2 * D :]], 1), jnp.concatenate(factors, 1)


def window(w):
    return pl.ds(pl.multiple_of(w * WT, WT), WT)


def attend(groups, step, qkv_ref, p_ref, scale2, factor, put, hmask, ones64):
    length, firsts = groups

    def scores(i, _):
        for n, first in enumerate(firsts):
            rows = window(first + i)
            for g in range(2):
                lanes = pl.ds(g * HALF, HALF)
                keys = spread(qkv_ref[rows, pl.ds(D + g * HALF, HALF)], hmask)
                e = jnp.exp2(mm_nt(qkv_ref[rows, lanes], keys) * scale2[:, g * GROUP : (g + 1) * GROUP])
                f = factor(n)
                p_ref[rows, pl.ds(g * GROUP, GROUP)] = (e if f is None else e * f).astype(BF16)
        return 0

    lax.fori_loop(0, length, scores, 0)
    total = length * len(firsts) * WT
    for i in range(total // step):
        rows = pl.ds(i * step, step)
        for g in range(2):
            lanes = pl.ds(g * GROUP, GROUP)
            e = p_ref[rows, lanes]
            s = mm(e, ones64)
            p_ref[rows, lanes] = (e.astype(F32) * pl.reciprocal(s)).astype(BF16)

    def mix(i, _):
        for first in firsts:
            rows = window(first + i)
            out = []
            for g in range(2):
                values = spread(qkv_ref[rows, pl.ds(2 * D + g * HALF, HALF)], hmask)
                out.append(mm(p_ref[rows, pl.ds(g * GROUP, GROUP)], values).astype(BF16))
            put(first + i, jnp.concatenate(out, 1))
        return 0

    lax.fori_loop(0, length, mix, 0)


def attend_back(groups, step, qkv_ref, p_ref, do_ref, ds_ref, dqkv_ref, scale, hmask, ones64):
    length, firsts = groups

    def probs(i, _):
        for first in firsts:
            rows = window(first + i)
            for g in range(2):
                values = spread(qkv_ref[rows, pl.ds(2 * D + g * HALF, HALF)], hmask)
                ds_ref[rows, pl.ds(g * GROUP, GROUP)] = mm_nt(do_ref[rows, pl.ds(g * HALF, HALF)], values).astype(BF16)
        return 0

    lax.fori_loop(0, length, probs, 0)
    total = length * len(firsts) * WT
    for i in range(total // step):
        rows = pl.ds(i * step, step)
        for g in range(2):
            lanes = pl.ds(g * GROUP, GROUP)
            p = p_ref[rows, lanes].astype(F32)
            pd = p * ds_ref[rows, lanes].astype(F32)
            ds = (pd - p * mm(pd.astype(BF16), ones64)) * scale[:, g * GROUP : (g + 1) * GROUP]
            ds_ref[rows, lanes] = ds.astype(BF16)

    def rest(i, _):
        for first in firsts:
            rows = window(first + i)
            for g in range(2):
                wide, lanes = pl.ds(g * GROUP, GROUP), pl.ds(g * HALF, HALF)
                ds, p = ds_ref[rows, wide], p_ref[rows, wide]
                keys = spread(qkv_ref[rows, pl.ds(D + g * HALF, HALF)], hmask)
                dqkv_ref[rows, lanes] = mm(ds, keys).astype(BF16)
                dqkv_ref[rows, pl.ds(D + g * HALF, HALF)] = gather_heads(mm_tn(ds, qkv_ref[rows, lanes])).astype(BF16)
                dqkv_ref[rows, pl.ds(2 * D + g * HALF, HALF)] = gather_heads(mm_tn(p, do_ref[rows, lanes])).astype(BF16)
        return 0

    lax.fori_loop(0, length, rest, 0)


def through_unit(dqkv, qkv, r, ones32):
    out = []
    for n in range(2):
        lanes = slice(n * D, (n + 1) * D)
        x, dn = qkv[:, lanes].astype(F32), dqkv[:, lanes].astype(F32)
        inner = mm((x * dn).astype(BF16), ones32)
        out.append((r[:, lanes].astype(F32) * (dn - x * inner)).astype(BF16))
    return jnp.concatenate(out + [dqkv[:, 2 * D :]], 1)


ROWS = 256


def feed(hm_ref, gain, wup_ref, wdown_ref, gp_ref, put):
    for i in range(T // ROWS):
        rows = pl.ds(i * ROWS, ROWS)
        h = hm_ref[rows, :]
        u = mm(norm(h, gain), wup_ref[...])
        c = 0.7978845608028654
        square = u * u
        t = jnp.tanh(u * (c + (c * 0.044715) * square))
        half = 0.5 + 0.5 * t
        gp_ref[rows, :] = (half + 0.5 * u * (1.0 - t * t) * (c + (3.0 * c * 0.044715) * square)).astype(BF16)
        put(i, rows, h + mm((u * half).astype(BF16), wdown_ref[...]))


def feed_back(rows, dh, hm_ref, gain, wup_ref, wdown_ref, gp_ref):
    dg = mm_nt(dh.astype(BF16), wdown_ref[...])
    du = (dg * gp_ref[rows, :].astype(F32)).astype(BF16)
    dn = mm_nt(du, wup_ref[...])
    return dh + norm_back(hm_ref[rows, :], gain, dn)


def route_kernel(owner_ref, count_ref, values_ref, aux_ref, out_ref, target_ref, wide_ref):
    step = 256
    upper = (
        lax.broadcasted_iota(jnp.int32, (step, step), 0) < lax.broadcasted_iota(jnp.int32, (step, step), 1)
    ).astype(BF16)
    carry = jnp.zeros((DEV, 1), F32)
    for i in range(OBS // step):
        owner = owner_ref[:, i * step : (i + 1) * step]
        live = (lax.broadcasted_iota(jnp.int32, (1, step), 1) + i * step) < count_ref[0]
        owner = jnp.where(live, owner, -1)
        hot = (lax.broadcasted_iota(jnp.int32, (DEV, step), 0) == owner).astype(F32)
        before = mm(hot.astype(BF16), upper) + carry
        carry = carry + jnp.sum(hot, 1, keepdims=True)
        place = jnp.sum(before * hot, 0, keepdims=True).astype(jnp.int32)
        target_ref[:, i * step : (i + 1) * step] = jnp.where(live, owner * CAP + place, -1)
    wide_ref[:, :CHAN] = values_ref[...].astype(BF16)
    wide_ref[:, CHAN:] = aux_ref[...]
    target = target_ref[...]
    row = lax.broadcasted_iota(jnp.int32, (step, OBS), 0)
    for i in range(SLOTS // step):
        pick = (row == target - i * step).astype(BF16)
        out_ref[pl.ds(i * step, step), :] = mm(pick, wide_ref[...]).astype(BF16)


def route(owner, point, count, values):
    patch = point // PIX
    lane = jnp.arange(DEV, dtype=jnp.int32)[None, :]
    place = jnp.where(lane == 0, (patch // PIX)[:, None], (patch % PIX)[:, None])
    place = jnp.where(lane == 2, (point % PIX)[:, None], place)
    place = jnp.where(lane == 3, 1, place)
    aux = jnp.where(lane < 4, place, 0).astype(BF16)
    return call(
        route_kernel,
        [((SLOTS, WIDE), BF16)],
        [pltpu.VMEM((1, OBS), jnp.int32), pltpu.VMEM((OBS, WIDE), BF16)],
        in_specs=[VMEM, SMEM, VMEM, VMEM],
    )(owner.reshape(1, OBS), count, values, aux)[0]


SIDES = [(-1, 0), (1, 0), (0, -1), (0, 1), (-1, -1), (-1, 1), (1, -1), (1, 1)]
SHAPES = [(6, 2), (6, 2), (2, 2), (2, 2), (), (), (), ()]
PACKED = (2, 6, 2, 2, BLK, D)


def edge(ref, side):
    r, c = side
    i, j = (0 if r < 0 else 1), (0 if c < 0 else 1)
    if c == 0:
        return ref.at[i, :, i]
    if r == 0:
        return ref.at[:, 5 * j, :, j]
    return ref.at[i, 5 * j, i, j]


def put_packed(ref, i, value):
    for k in range(ROWS // WT):
        w = i * (ROWS // WT) + k
        ref[w // 6, w % 6] = value[k * WT : (k + 1) * WT].reshape(2, 2, BLK, D)


def neighbour(n_lat, n_lon, side):
    lat, lon = lax.axis_index("lat"), lax.axis_index("lon")
    return (lax.rem(lat + side[0] + n_lat, n_lat), lax.rem(lon + side[1] + n_lon, n_lon))


def swap_edges(n_lat, n_lon, z_ref, halos, send, recv):
    copies = []
    for n, side in enumerate(SIDES):
        opposite = SIDES.index((-side[0], -side[1]))
        copies.append(
            pltpu.make_async_remote_copy(
                src_ref=edge(z_ref, side),
                dst_ref=halos[opposite],
                send_sem=send.at[n],
                recv_sem=recv.at[opposite],
                device_id=neighbour(n_lat, n_lon, side),
                device_id_type=pl.DeviceIdType.MESH,
            )
        )
        copies[-1].start()
    return copies


def shifted_blocks():
    for si in range(SW_R):
        for sj in range(SW_C):
            for k in range(4):
                yield ((si * SW_C + sj) * 4 + k) * BLK, 2 * si - 1 + k // 2, 2 * sj - 1 + k % 2


def inside(bi, bj):
    return 0 <= bi < BR and 0 <= bj < BC


def outer(out_ref, halos):
    for n, (_, bi, bj) in enumerate(outer_blocks()):
        r = -1 if bi < 0 else 1 if bi >= BR else 0
        c = -1 if bj < 0 else 1 if bj >= BC else 0
        halo = halos[SIDES.index((r, c))]
        if c == 0:
            value = halo[bj // 2, bj % 2]
        elif r == 0:
            value = halo[bi // 2, bi % 2]
        else:
            value = halo[...]
        out_ref[pl.ds(n * BLK, BLK), :] = value


def outer_blocks():
    return [b for b in shifted_blocks() if not inside(b[1], b[2])]


TO = len(outer_blocks()) * BLK


FETCHED = ["state", "wemb", "wqkv", "wproj", "wup", "wdown", "recv", "w1", "w2", "rinv", "whead", "background"]


def whole_kernel(
    n_lat, n_lon, gain_ref, scale_ref, order_ref, place_ref, pixel_ref, inverse_ref, *refs,
):
    n = len(FETCHED)
    source = dict(zip(FETCHED, refs[:n]))
    part_out, d0_out = refs[n : n + 2]
    refs = refs[n + 2 :]
    held = dict(zip(FETCHED, refs[:n]))
    (sb, h0, hm0, h1, hm1, z1, qkv0, qkv1, r0, r1, p0, p1, gp0, gp1, o, zo, qo, hot, adj, gm) = refs[n : n + 20]
    halo_z, halo_a = refs[n + 20 : n + 28], refs[n + 28 : n + 36]
    fetch_sem, out_sem, send_z, recv_z, send_a, recv_a = refs[n + 36 :]
    fetches = {name: pltpu.make_async_copy(source[name], held[name], fetch_sem.at[k]) for k, name in enumerate(FETCHED)}
    for name in FETCHED:
        fetches[name].start()
    barrier = pltpu.get_barrier_semaphore()
    for side in SIDES:
        pl.semaphore_signal(
            barrier, inc=1, device_id=neighbour(n_lat, n_lon, side), device_id_type=pl.DeviceIdType.MESH
        )
    ones32, ones64, hmask = same_group(D, D // HEADS), same_group(GROUP, WT), head_mask()
    log2e = 1.4426950408889634
    scale0, scale1 = scale_ref[0:1, :], scale_ref[1:2, :]
    plain = (T // WT // 3, [0, 4, 8])
    shifted = (SW_C, [0, SW_C, 2 * SW_C])

    perm = permutation(order_ref[...])
    fetches["state"].wait()
    sb[...] = held["state"][...].astype(BF16)
    fetches["wemb"].wait()
    fetches["wqkv"].wait()
    for i in range(T // ROWS):
        rows = pl.ds(i * ROWS, ROWS)
        mine = mm(perm[i * ROWS : (i + 1) * ROWS], sb[...]).astype(BF16)
        hidden = mm(mine, held["wemb"][...])
        h0[rows, :] = hidden
        qkv0[rows, :], r0[rows, :] = project(norm(hidden, gain_ref[0, 0:1, :]), held["wqkv"][0], ones32)

    def put_o(w, value):
        o[window(w), :] = value

    attend(plain, ROWS, qkv0, p0, scale0 * log2e, lambda n: None, put_o, hmask, ones64)
    fetches["wproj"].wait()
    fetches["wup"].wait()
    fetches["wdown"].wait()
    hm0[...] = h0[...] + mm(o[pl.ds(0, T), :], held["wproj"][0]).astype(BF16).astype(F32)

    def put_first(i, rows, value):
        h1[rows, :] = value
        put_packed(z1, i, norm(value, gain_ref[1, 0:1, :]))

    feed(hm0, gain_ref[0, 1:2, :], held["wup"].at[0], held["wdown"].at[0], gp0, put_first)

    pl.semaphore_wait(barrier, 8)
    copies = swap_edges(n_lat, n_lon, z1, halo_z, send_z, recv_z)
    for i in range(T // ROWS):
        for k in range(ROWS // WT):
            w = i * (ROWS // WT) + k
            o[pl.ds(w * WT, WT), :] = z1[w // 6, w % 6].reshape(WT, D)
        rows = pl.ds(i * ROWS, ROWS)
        qo[rows, :], zo[rows, :] = project(o[rows, :], held["wqkv"][1], ones32)
    for row, bi, bj in shifted_blocks():
        if inside(bi, bj):
            qkv1[pl.ds(row, BLK), :] = qo[pl.ds(block_at(bi, bj), BLK), :]
            r1[pl.ds(row, BLK), :] = zo[pl.ds(block_at(bi, bj), BLK), :]
    for copy in copies:
        copy.wait()
    outer(o, halo_z)
    for i in range(2):
        rows = pl.ds(i * (TO // 2), TO // 2)
        qo[rows, :], _ = project(o[rows, :], held["wqkv"][1], ones32)
    for k, (row, _, _) in enumerate(outer_blocks()):
        qkv1[pl.ds(row, BLK), :] = qo[pl.ds(k * BLK, BLK), :]
    a = lax.broadcasted_iota(jnp.int32, (WT, GROUP), 0) // (2 * BLK)
    b = lax.broadcasted_iota(jnp.int32, (WT, GROUP), 1) // (2 * BLK) % 2
    apart = (a != b).astype(F32)
    lat = lax.axis_index("lat")
    top = 1.0 - apart * (lat == 0).astype(F32)
    bottom = 1.0 - apart * (lat == n_lat - 1).astype(F32)
    attend(shifted, TX // 3, qkv1, p1, scale1 * log2e, lambda n: (top, None, bottom)[n], put_o, hmask, ones64)
    for row, bi, bj in shifted_blocks():
        if inside(bi, bj):
            zo[pl.ds(block_at(bi, bj), BLK), :D] = o[pl.ds(row, BLK), :]
    hm1[...] = h1[...] + mm(zo[:, :D], held["wproj"][1]).astype(BF16).astype(F32)

    def put_second(i, rows, value):
        zo[rows, :D] = value.astype(BF16)

    feed(hm1, gain_ref[1, 1:2, :], held["wup"].at[1], held["wdown"].at[1], gp1, put_second)
    back = permutation(place_ref[...])
    fetches["whead"].wait()
    for i in range(T // ROWS):
        rows = pl.ds(i * ROWS, ROWS)
        mine = mm(back[i * ROWS : (i + 1) * ROWS], zo[:, :D]).astype(BF16)
        sb[rows, :] = (held["state"][rows, :] + mm_nt(mine, held["whead"][...])).astype(BF16)

    for name in ("recv", "w1", "w2", "rinv", "background"):
        fetches[name].wait()
    radiance(held["recv"], sb, pixel_ref[...], held["w1"], held["w2"][...], held["rinv"][...], hot, adj)
    for i in range(T // ROWS):
        rows = pl.ds(i * ROWS, ROWS)
        value = mm(hot[rows, :], adj[...])
        gm[rows, :] = value + inverse_ref[...] * (held["state"][rows, :] - held["background"][rows, :])
        zo[rows, :D] = mm(value.astype(BF16), held["whead"][...]).astype(BF16)
    part = pltpu.make_async_copy(gm, part_out, out_sem)
    part.start()

    perm = permutation(order_ref[...])
    for i in range(T // ROWS):
        rows = pl.ds(i * ROWS, ROWS)
        d3 = mm(perm[i * ROWS : (i + 1) * ROWS], zo[:, :D])
        d2 = feed_back(rows, d3, hm1, gain_ref[1, 1:2, :], held["wup"].at[1], held["wdown"].at[1], gp1)
        hm1[rows, :] = d2
        put_packed(z1, i, d2.astype(BF16))
    copies = swap_edges(n_lat, n_lon, z1, halo_a, send_a, recv_a)
    wp = held["wproj"][1]
    for w in range(T // WT):
        zo[pl.ds(w * WT, WT), :D] = z1[w // 6, w % 6].reshape(WT, D)
    zo[:, D:] = mm_nt(zo[:, :D], wp).astype(BF16)
    for row, bi, bj in shifted_blocks():
        if inside(bi, bj):
            o[pl.ds(row, BLK), :] = zo[pl.ds(block_at(bi, bj), BLK), D:]
    for copy in copies:
        copy.wait()
    outer(zo.at[:, :D], halo_a)
    zo[pl.ds(0, TO), D:] = mm_nt(zo[pl.ds(0, TO), :D], wp).astype(BF16)
    for k, (row, _, _) in enumerate(outer_blocks()):
        o[pl.ds(row, BLK), :] = zo[pl.ds(k * BLK, BLK), D:]
    whole_back(
        shifted, plain, ones32, ones64, hmask, scale0, scale1, gain_ref, held, h0, hm0, h1, hm1,
        qkv0, qkv1, r0, r1, p0, p1, gp0, o, zo, qo, adj,
    )
    back = permutation(place_ref[...])
    for i in range(T // ROWS):
        rows = pl.ds(i * ROWS, ROWS)
        d0_out[rows, :] = mm(back[i * ROWS : (i + 1) * ROWS], zo[:, :D]).astype(BF16)
    part.wait()


def whole_back(
    shifted, plain, ones32, ones64, hmask, scale0, scale1, gain_ref, held, h0, hm0, h1, hm1,
    qkv0, qkv1, r0, r1, p0, p1, gp0, o, zo, qo, adj,
):
    ds = adj.at[pl.ds(0, TX), pl.ds(0, 2 * GROUP)]
    dqkv = adj.at[pl.ds(TX, TX), pl.ds(0, 3 * D)]
    attend_back(shifted, TX // 3, qkv1, p1, o, ds, dqkv, scale1, hmask, ones64)
    step = TX // 3
    for i in range(3):
        rows = pl.ds(i * step, step)
        dqkv[rows, :] = through_unit(dqkv[rows, :], qkv1[rows, :], r1[rows, :], ones32)
    for row, bi, bj in shifted_blocks():
        if inside(bi, bj):
            qo[pl.ds(block_at(bi, bj), BLK), :] = dqkv[pl.ds(row, BLK), :]
    for i in range(T // ROWS):
        rows = pl.ds(i * ROWS, ROWS)
        dz = mm_nt(qo[rows, :], held["wqkv"][1])
        d1 = hm1[rows, :] + norm_back(h1[rows, :], gain_ref[1, 0:1, :], dz)
        dm = feed_back(rows, d1, hm0, gain_ref[0, 1:2, :], held["wup"].at[0], held["wdown"].at[0], gp0)
        hm1[rows, :] = dm
        o[rows, :] = mm_nt(dm.astype(BF16), held["wproj"][0]).astype(BF16)
    attend_back(plain, ROWS, qkv0, p0, o, ds, dqkv, scale0, hmask, ones64)
    for i in range(T // ROWS):
        rows = pl.ds(i * ROWS, ROWS)
        dz = mm_nt(through_unit(dqkv[rows, :], qkv0[rows, :], r0[rows, :], ones32), held["wqkv"][0])
        zo[rows, :D] = (hm1[rows, :] + norm_back(h0[rows, :], gain_ref[0, 0:1, :], dz)).astype(BF16)


def radiance(recv_ref, moved_ref, pixel, w1_ref, w2, rinv, hot_ref, adj_ref):
    step = 256
    pick = (
        lax.broadcasted_iota(jnp.int32, (8, DEV), 0) == lax.broadcasted_iota(jnp.int32, (8, DEV), 1)
    ).astype(BF16)
    lane = lax.broadcasted_iota(jnp.int32, (step, T), 1)
    row = lax.broadcasted_iota(jnp.int32, (T, step), 0)
    w2, rinv = w2.astype(BF16), rinv.astype(BF16)

    def chunk(i):
        rows = pl.ds(pl.multiple_of(i * step, step), step)
        aux16 = recv_ref[rows, CHAN:]
        aux = aux16.astype(F32)
        live = aux[:, 3:4]
        patch = jnp.where(live > 0, aux[:, 0:1] * PIX + aux[:, 1:2], -1.0).astype(jnp.int32)
        hot = (lane == patch).astype(BF16)
        flat = mm_nt(pick, aux16)
        across = jnp.where(flat[3:4] > 0, flat[0:1] * PIX + flat[1:2], -1.0).astype(jnp.int32)
        hot_ref[:, rows] = (row == across).astype(BF16)
        here = pixel == aux[:, 2:3]
        found = jnp.where(here, mm(hot, moved_ref[...]), 0.0).astype(BF16)
        inner = jnp.tanh(mm(found, w1_ref[...]))
        innovation = (mm(inner.astype(BF16), w2) - recv_ref[rows, :CHAN].astype(F32)) * live
        weighted = mm(innovation.astype(BF16), rinv).astype(BF16)
        pulled = mm_nt(weighted, w2) * (1.0 - inner * inner)
        adj_ref[rows, :] = jnp.where(here, mm_nt(pulled.astype(BF16), w1_ref[...]), 0.0).astype(BF16)

    def chunks(i, _):
        chunk(2 * i)
        chunk(2 * i + 1)
        return 0

    lax.fori_loop(0, SLOTS // step // 2, chunks, 0)


def whole(n_lat, n_lon, small, fetched):
    halo = [pltpu.VMEM(s + (BLK, D), BF16) for s in SHAPES]
    ANY = pl.BlockSpec(memory_space=pl.ANY)
    scratch = [pltpu.VMEM(a.shape, a.dtype) for a in fetched]
    scratch += [
        pltpu.VMEM(s, d)
        for s, d in [
            ((T, PV), BF16), ((T, D), F32), ((T, D), F32), ((T, D), F32), ((T, D), F32), (PACKED, BF16),
            ((T, 3 * D), BF16), ((TX, 3 * D), BF16), ((T, 2 * D), BF16), ((TX, 2 * D), BF16),
            ((T, 2 * GROUP), BF16), ((TX, 2 * GROUP), BF16), ((T, FFN), BF16), ((T, FFN), BF16),
            ((TX, D), BF16), ((T, 2 * D), BF16), ((T, 3 * D), BF16),
            ((T, SLOTS), BF16), ((SLOTS, PV), BF16), ((T, PV), F32),
        ]
    ]
    scratch += halo + halo
    scratch += [pltpu.SemaphoreType.DMA((len(fetched),)), pltpu.SemaphoreType.DMA]
    scratch += [pltpu.SemaphoreType.DMA((8,))] * 4
    return pl.pallas_call(
        functools.partial(whole_kernel, n_lat, n_lon),
        out_shape=[jax.ShapeDtypeStruct((T, PV), F32), jax.ShapeDtypeStruct((T, D), BF16)],
        in_specs=[VMEM] * len(small) + [ANY] * len(fetched),
        out_specs=[ANY, VMEM],
        scratch_shapes=scratch,
        compiler_params=pltpu.CompilerParams(vmem_limit_bytes=60 << 20, collective_id=1, has_side_effects=True),
    )(*small, *fetched)


def last_kernel(d0_ref, wemb_ref, part_ref, out_ref):
    out_ref[...] = part_ref[...] + mm_nt(d0_ref[...], wemb_ref[...])


def last(d0, w_embed, part):
    step = 128
    piece = pl.BlockSpec((step, PV), lambda i: (i, 0))
    return pl.pallas_call(
        last_kernel,
        grid=(T // step,),
        out_shape=jax.ShapeDtypeStruct((T, PV), F32),
        in_specs=[pl.BlockSpec((step, D), lambda i: (i, 0)), pl.BlockSpec((PV, D), lambda i: (0, 0)), piece],
        out_specs=piece,
        compiler_params=pltpu.CompilerParams(vmem_limit_bytes=16 << 20),
    )(d0, w_embed, part)


def local(
    n_lat, n_lon, state, background, inv_background, w_embed, norm_gain, w_qkv, w_proj, head_scale, w_up,
    w_down, w_head, w_obs1, w_obs2, r_inverse, obs_values, obs_owner, obs_point, obs_count,
):
    order = jnp.asarray(ORDER).reshape(T, 1)
    place = jnp.asarray(PLACE).reshape(T, 1)
    scales = jnp.repeat(head_scale, WT, axis=1)
    w1 = jnp.tile(w_obs1.astype(BF16), (PIX, 1))
    pixel = (jnp.arange(PV, dtype=jnp.int32) // VARS).astype(F32).reshape(1, PV)
    sent = route(obs_owner, obs_point, obs_count, obs_values)
    recv = lax.all_to_all(
        sent.reshape(DEV, CAP, WIDE), ("lat", "lon"), split_axis=0, concat_axis=0, tiled=True
    ).reshape(SLOTS, WIDE)
    small = [norm_gain, scales, order, place, pixel, inv_background.reshape(1, PV)]
    fetched = [
        state.reshape(T, PV), w_embed, w_qkv, w_proj, w_up, w_down, recv, w1, w_obs2, r_inverse, w_head.T,
        background.reshape(T, PV),
    ]
    part, d0 = whole(n_lat, n_lon, small, fetched)
    return last(d0, w_embed, part).reshape(state.shape)


def solution(mesh):
    grid = P("lat", "lon", None)
    slots = P(("lat", "lon"))
    placed = (grid, grid) + (P(),) * 12 + (P(("lat", "lon"), None),) * 2 + (slots, slots)
    return jax.shard_map(
        functools.partial(local, mesh.shape["lat"], mesh.shape["lon"]),
        mesh=mesh,
        in_specs=placed,
        out_specs=grid,
        check_vma=False,
    )
```

```python
import functools

import jax
import jax.numpy as jnp
import numpy as np
from jax import lax
from jax.experimental import pallas as pl
from jax.experimental.pallas import tpu as pltpu
from jax.sharding import PartitionSpec as P

F32 = jnp.float32
BF16 = jnp.bfloat16
EPS = 1e-05
VARS = 69
PIX = 16
HEADS = 8
D = 256
FFN = 1024
PV = 1104
T = 768
BLK = 16
WT = 64
BR, BC = 4, 12
SW_R, SW_C = 3, 7
TX = SW_R * SW_C * WT
CAP = 32
DEV = 128
SLOTS = DEV * CAP
OBS = 2048
CHAN = 256
WIDE = 384
VMEM = pl.BlockSpec(memory_space=pltpu.VMEM)
SMEM = pl.BlockSpec(memory_space=pltpu.SMEM)


def mm(a, b):
    return jnp.dot(a, b, preferred_element_type=F32)


def mm_nt(a, b):
    return lax.dot_general(a, b, (((1,), (1,)), ((), ())), preferred_element_type=F32)


def mm_tn(a, b):
    return lax.dot_general(a, b, (((0,), (0,)), ((), ())), preferred_element_type=F32)


def block_at(bi, bj):
    return (((bi // 2) * (BC // 2) + bj // 2) * 4 + (bi % 2) * 2 + bj % 2) * BLK


def row_of_place():
    out = np.zeros((T,), np.int32)
    for bi in range(BR):
        for bj in range(BC):
            for k in range(BLK):
                out[block_at(bi, bj) + k] = (bi * 4 + k // 4) * (BC * 4) + bj * 4 + k % 4
    return out


ORDER = row_of_place()
PLACE = np.argsort(ORDER).astype(np.int32)


def permutation(column):
    return (lax.broadcasted_iota(jnp.int32, (T, T), 1) == column).astype(BF16)


def norm_parts(x):
    centred = x - jnp.mean(x, -1, keepdims=True)
    scale = lax.rsqrt(jnp.mean(centred * centred, -1, keepdims=True) + EPS)
    return centred * scale, scale


def norm(x, gain):
    return (norm_parts(x)[0] * gain).astype(BF16)


def norm_back(x, gain, dy):
    unit, scale = norm_parts(x)
    dn = dy * gain
    return scale * (dn - jnp.mean(dn, -1, keepdims=True) - unit * jnp.mean(dn * unit, -1, keepdims=True))


def same_group(n, size):
    a = lax.broadcasted_iota(jnp.int32, (n, n), 0) // size
    b = lax.broadcasted_iota(jnp.int32, (n, n), 1) // size
    return (a == b).astype(BF16)


HALF = D // 2
GROUP = 4 * WT


def head_mask():
    a = lax.broadcasted_iota(jnp.int32, (GROUP, HALF), 0) // WT
    b = lax.broadcasted_iota(jnp.int32, (GROUP, HALF), 1) // (D // HEADS)
    return (a == b).astype(BF16)


def spread(x, hmask):
    return jnp.concatenate([x] * 4, 0) * hmask


def gather_heads(x):
    lane = lax.broadcasted_iota(jnp.int32, (WT, HALF), 1) // (D // HEADS)
    out = x[:WT]
    for h in range(1, 4):
        out = jnp.where(lane == h, x[h * WT : (h + 1) * WT], out)
    return out


def project(z, wqkv, ones32):
    qkv = mm(z, wqkv).astype(BF16)
    parts, factors = [], []
    for n in range(2):
        x = qkv[:, n * D : (n + 1) * D].astype(F32)
        r = lax.rsqrt(mm((x * x).astype(BF16), ones32) + 1.0)
        parts.append((x * r).astype(BF16))
        factors.append(r.astype(BF16))
    return jnp.concatenate(parts + [qkv[:, 2 * D :]], 1), jnp.concatenate(factors, 1)


def window(w):
    return pl.ds(pl.multiple_of(w * WT, WT), WT)


def attend(groups, step, qkv_ref, p_ref, scale2, factor, put, hmask, ones64):
    length, firsts = groups

    def scores(i, _):
        for n, first in enumerate(firsts):
            rows = window(first + i)
            for g in range(2):
                lanes = pl.ds(g * HALF, HALF)
                keys = spread(qkv_ref[rows, pl.ds(D + g * HALF, HALF)], hmask)
                e = jnp.exp2(mm_nt(qkv_ref[rows, lanes], keys) * scale2[:, g * GROUP : (g + 1) * GROUP])
                f = factor(n)
                p_ref[rows, pl.ds(g * GROUP, GROUP)] = (e if f is None else e * f).astype(BF16)
        return 0

    lax.fori_loop(0, length, scores, 0)
    total = length * len(firsts) * WT
    for i in range(total // step):
        rows = pl.ds(i * step, step)
        for g in range(2):
            lanes = pl.ds(g * GROUP, GROUP)
            e = p_ref[rows, lanes]
            s = mm(e, ones64)
            p_ref[rows, lanes] = (e.astype(F32) * pl.reciprocal(s)).astype(BF16)

    def mix(i, _):
        for first in firsts:
            rows = window(first + i)
            out = []
            for g in range(2):
                values = spread(qkv_ref[rows, pl.ds(2 * D + g * HALF, HALF)], hmask)
                out.append(mm(p_ref[rows, pl.ds(g * GROUP, GROUP)], values).astype(BF16))
            put(first + i, jnp.concatenate(out, 1))
        return 0

    lax.fori_loop(0, length, mix, 0)


def attend_back(groups, step, qkv_ref, p_ref, do_ref, ds_ref, dqkv_ref, scale, hmask, ones64):
    length, firsts = groups

    def probs(i, _):
        for first in firsts:
            rows = window(first + i)
            for g in range(2):
                values = spread(qkv_ref[rows, pl.ds(2 * D + g * HALF, HALF)], hmask)
                ds_ref[rows, pl.ds(g * GROUP, GROUP)] = mm_nt(do_ref[rows, pl.ds(g * HALF, HALF)], values).astype(BF16)
        return 0

    lax.fori_loop(0, length, probs, 0)
    total = length * len(firsts) * WT
    for i in range(total // step):
        rows = pl.ds(i * step, step)
        for g in range(2):
            lanes = pl.ds(g * GROUP, GROUP)
            p = p_ref[rows, lanes].astype(F32)
            pd = p * ds_ref[rows, lanes].astype(F32)
            ds = (pd - p * mm(pd.astype(BF16), ones64)) * scale[:, g * GROUP : (g + 1) * GROUP]
            ds_ref[rows, lanes] = ds.astype(BF16)

    def rest(i, _):
        for first in firsts:
            rows = window(first + i)
            for g in range(2):
                wide, lanes = pl.ds(g * GROUP, GROUP), pl.ds(g * HALF, HALF)
                ds, p = ds_ref[rows, wide], p_ref[rows, wide]
                keys = spread(qkv_ref[rows, pl.ds(D + g * HALF, HALF)], hmask)
                dqkv_ref[rows, lanes] = mm(ds, keys).astype(BF16)
                dqkv_ref[rows, pl.ds(D + g * HALF, HALF)] = gather_heads(mm_tn(ds, qkv_ref[rows, lanes])).astype(BF16)
                dqkv_ref[rows, pl.ds(2 * D + g * HALF, HALF)] = gather_heads(mm_tn(p, do_ref[rows, lanes])).astype(BF16)
        return 0

    lax.fori_loop(0, length, rest, 0)


def through_unit(dqkv, qkv, r, ones32):
    out = []
    for n in range(2):
        lanes = slice(n * D, (n + 1) * D)
        x, dn = qkv[:, lanes].astype(F32), dqkv[:, lanes].astype(F32)
        inner = mm((x * dn).astype(BF16), ones32)
        out.append((r[:, lanes].astype(F32) * (dn - x * inner)).astype(BF16))
    return jnp.concatenate(out + [dqkv[:, 2 * D :]], 1)


ROWS = 256


def feed(hm_ref, gain, wup_ref, wdown_ref, gp_ref, put):
    for i in range(T // ROWS):
        rows = pl.ds(i * ROWS, ROWS)
        h = hm_ref[rows, :]
        u = mm(norm(h, gain), wup_ref[...])
        c = 0.7978845608028654
        square = u * u
        t = jnp.tanh(u * (c + (c * 0.044715) * square))
        half = 0.5 + 0.5 * t
        gp_ref[rows, :] = (half + 0.5 * u * (1.0 - t * t) * (c + (3.0 * c * 0.044715) * square)).astype(BF16)
        put(i, rows, h + mm((u * half).astype(BF16), wdown_ref[...]))


def feed_back(rows, dh, hm_ref, gain, wup_ref, wdown_ref, gp_ref):
    dg = mm_nt(dh.astype(BF16), wdown_ref[...])
    du = (dg * gp_ref[rows, :].astype(F32)).astype(BF16)
    dn = mm_nt(du, wup_ref[...])
    return dh + norm_back(hm_ref[rows, :], gain, dn)


CHUNK = 256
OWNERS = CHUNK // CAP


def other(n_lon, n):
    return (n // n_lon, lax.rem(n, n_lon))


def route(n_lon, me, owner_ref, point_ref, count, values_ref, target_ref, wide_ref, out_ref, aux_ref, recv, recv_aux, sems):
    upper = (
        lax.broadcasted_iota(jnp.int32, (CHUNK, CHUNK), 0) < lax.broadcasted_iota(jnp.int32, (CHUNK, CHUNK), 1)
    ).astype(BF16)
    carry = jnp.zeros((DEV, 1), F32)
    for i in range(OBS // CHUNK):
        lanes = pl.ds(i * CHUNK, CHUNK)
        live = (lax.broadcasted_iota(jnp.int32, (1, CHUNK), 1) + i * CHUNK) < count
        owner = jnp.where(live, owner_ref[:, lanes], -1)
        hot = (lax.broadcasted_iota(jnp.int32, (DEV, CHUNK), 0) == owner).astype(F32)
        before = mm(hot.astype(BF16), upper) + carry
        carry = carry + jnp.sum(hot, 1, keepdims=True)
        place = jnp.sum(before * hot, 0, keepdims=True).astype(jnp.int32)
        target_ref[:, lanes] = jnp.where(live, owner * CAP + place, -1)
    wide_ref[...] = values_ref[...].astype(BF16)
    point = point_ref[...]
    kind = lax.broadcasted_iota(jnp.int32, (16, OBS), 0)
    place = jnp.where(kind == 0, point // (PIX * PIX), jnp.where(kind == 1, point // PIX % PIX, point % PIX))
    place = jnp.where(kind < 3, place, jnp.where(kind == 3, 1, 0)).astype(F32).astype(BF16)
    row = lax.broadcasted_iota(jnp.int32, (CHUNK, OBS), 0)

    def remote(src, dst, n, k):
        return pltpu.make_async_remote_copy(
            src_ref=src, dst_ref=dst, send_sem=sems.at[k], recv_sem=sems.at[2 + k],
            device_id=other(n_lon, n), device_id_type=pl.DeviceIdType.MESH,
        )

    def chunk(i, _):
        c = lax.rem(i + me // OWNERS, DEV // OWNERS)
        base = pl.multiple_of(c * CHUNK, CHUNK)
        pick = (row == target_ref[...] - base).astype(BF16)
        out_ref[pl.ds(base, CHUNK), pl.ds(0, CHAN)] = mm(pick, wide_ref[...]).astype(BF16)
        across = mm_nt(place, pick).astype(BF16)
        for j in range(OWNERS):
            n = c * OWNERS + j
            mine = across[:, j * CAP : (j + 1) * CAP]
            aux_ref[n] = jnp.concatenate([mine, jnp.zeros((16, DEV - CAP), BF16)], 1)
        for j in range(OWNERS):
            n = c * OWNERS + j
            block = out_ref.at[pl.ds(pl.multiple_of(n * CAP, CAP), CAP), pl.ds(0, CHAN)]

            @pl.when(n != me)
            def _():
                remote(block, recv.at[me], n, 0).start()
                remote(aux_ref.at[n], recv_aux.at[me], n, 1).start()

        return 0

    lax.fori_loop(0, SLOTS // CHUNK, chunk, 0)
    block = out_ref.at[pl.ds(pl.multiple_of(me * CAP, CAP), CAP), pl.ds(0, CHAN)]
    kept = [
        pltpu.make_async_copy(block, recv.at[me], sems.at[4]),
        pltpu.make_async_copy(aux_ref.at[me], recv_aux.at[me], sems.at[5]),
    ]
    for copy in kept:
        copy.start()
    return kept


def routed(kept, recv, recv_aux, sems):
    for copy in kept:
        copy.wait()
    for k in range(2):
        for ref, n in ((recv, 0), (recv_aux, 1)):
            part = ref.at[pl.ds(0, DEV - 1)]
            pltpu.make_async_copy(part, part, sems.at[2 * k + n]).wait()


SIDES = [(-1, 0), (1, 0), (0, -1), (0, 1), (-1, -1), (-1, 1), (1, -1), (1, 1)]
SHAPES = [(6, 2), (6, 2), (2, 2), (2, 2), (), (), (), ()]
PACKED = (2, 6, 2, 2, BLK, D)


def edge(ref, side):
    r, c = side
    i, j = (0 if r < 0 else 1), (0 if c < 0 else 1)
    if c == 0:
        return ref.at[i, :, i]
    if r == 0:
        return ref.at[:, 5 * j, :, j]
    return ref.at[i, 5 * j, i, j]


def put_packed(ref, i, value):
    for k in range(ROWS // WT):
        w = i * (ROWS // WT) + k
        ref[w // 6, w % 6] = value[k * WT : (k + 1) * WT].reshape(2, 2, BLK, D)


def neighbour(n_lat, n_lon, side):
    lat, lon = lax.axis_index("lat"), lax.axis_index("lon")
    return (lax.rem(lat + side[0] + n_lat, n_lat), lax.rem(lon + side[1] + n_lon, n_lon))


def swap_edges(n_lat, n_lon, z_ref, halos, send, recv):
    copies = []
    for n, side in enumerate(SIDES):
        opposite = SIDES.index((-side[0], -side[1]))
        copies.append(
            pltpu.make_async_remote_copy(
                src_ref=edge(z_ref, side),
                dst_ref=halos[opposite],
                send_sem=send.at[n],
                recv_sem=recv.at[opposite],
                device_id=neighbour(n_lat, n_lon, side),
                device_id_type=pl.DeviceIdType.MESH,
            )
        )
        copies[-1].start()
    return copies


def shifted_blocks():
    for si in range(SW_R):
        for sj in range(SW_C):
            for k in range(4):
                yield ((si * SW_C + sj) * 4 + k) * BLK, 2 * si - 1 + k // 2, 2 * sj - 1 + k % 2


def inside(bi, bj):
    return 0 <= bi < BR and 0 <= bj < BC


def outer(out_ref, halos):
    for n, (_, bi, bj) in enumerate(outer_blocks()):
        r = -1 if bi < 0 else 1 if bi >= BR else 0
        c = -1 if bj < 0 else 1 if bj >= BC else 0
        halo = halos[SIDES.index((r, c))]
        if c == 0:
            value = halo[bj // 2, bj % 2]
        elif r == 0:
            value = halo[bi // 2, bi % 2]
        else:
            value = halo[...]
        out_ref[pl.ds(n * BLK, BLK), :] = value


def outer_blocks():
    return [b for b in shifted_blocks() if not inside(b[1], b[2])]


TO = len(outer_blocks()) * BLK


FETCHED = ["values", "state", "wemb", "wqkv", "wproj", "wup", "wdown", "w1", "w2", "rinv", "whead", "background"]


def whole_kernel(
    n_lat, n_lon, count_ref, owner_ref, point_ref, gain_ref, scale_ref, order_ref, place_ref, pixel_ref, inverse_ref,
    *refs,
):
    n = len(FETCHED)
    source = dict(zip(FETCHED, refs[:n]))
    result = refs[n]
    refs = refs[n + 1 :]
    held = dict(zip(FETCHED, refs[:n]))
    (sb, h0, hm0, h1, hm1, z1, qkv0, qkv1, r0, r1, p0, p1, gp0, gp1, o, zo, qo, hot, adj, gm) = refs[n : n + 20]
    halo_z, halo_a = refs[n + 20 : n + 28], refs[n + 28 : n + 36]
    recv, recv_aux, send_aux, target, wide, w1, fetch_sem, out_sem, send_z, recv_z, send_a, recv_a, sems = refs[n + 36 :]
    fetches = {name: pltpu.make_async_copy(source[name], held[name], fetch_sem.at[k]) for k, name in enumerate(FETCHED)}
    for name in FETCHED:
        fetches[name].start()
    barrier = pltpu.get_barrier_semaphore()
    me = lax.axis_index("lat") * n_lon + lax.axis_index("lon")

    def greet(k, _):
        pl.semaphore_signal(
            barrier, inc=1, device_id=other(n_lon, lax.rem(me + k, DEV)), device_id_type=pl.DeviceIdType.MESH
        )
        return 0

    lax.fori_loop(1, DEV, greet, 0)
    ones32, ones64, hmask = same_group(D, D // HEADS), same_group(GROUP, WT), head_mask()
    log2e = 1.4426950408889634
    scale0, scale1 = scale_ref[0:1, :], scale_ref[1:2, :]
    plain = (T // WT // 3, [0, 4, 8])
    shifted = (SW_C, [0, SW_C, 2 * SW_C])

    fetches["values"].wait()
    pl.semaphore_wait(barrier, DEV - 1)
    kept = route(
        n_lon, me, owner_ref, point_ref, count_ref[0], held["values"], target, wide, adj, send_aux, recv, recv_aux, sems
    )

    perm = permutation(order_ref[...])
    fetches["state"].wait()
    sb[...] = held["state"][...].astype(BF16)
    fetches["wemb"].wait()
    fetches["wqkv"].wait()
    for i in range(T // ROWS):
        rows = pl.ds(i * ROWS, ROWS)
        mine = mm(perm[i * ROWS : (i + 1) * ROWS], sb[...]).astype(BF16)
        hidden = mm(mine, held["wemb"][...])
        h0[rows, :] = hidden
        qkv0[rows, :], r0[rows, :] = project(norm(hidden, gain_ref[0, 0:1, :]), held["wqkv"][0], ones32)

    def put_o(w, value):
        o[window(w), :] = value

    attend(plain, ROWS, qkv0, p0, scale0 * log2e, lambda n: None, put_o, hmask, ones64)
    fetches["wproj"].wait()
    fetches["wup"].wait()
    fetches["wdown"].wait()
    hm0[...] = h0[...] + mm(o[pl.ds(0, T), :], held["wproj"][0]).astype(BF16).astype(F32)

    def put_first(i, rows, value):
        h1[rows, :] = value
        put_packed(z1, i, norm(value, gain_ref[1, 0:1, :]))

    feed(hm0, gain_ref[0, 1:2, :], held["wup"].at[0], held["wdown"].at[0], gp0, put_first)

    copies = swap_edges(n_lat, n_lon, z1, halo_z, send_z, recv_z)
    for i in range(T // ROWS):
        for k in range(ROWS // WT):
            w = i * (ROWS // WT) + k
            o[pl.ds(w * WT, WT), :] = z1[w // 6, w % 6].reshape(WT, D)
        rows = pl.ds(i * ROWS, ROWS)
        qo[rows, :], zo[rows, :] = project(o[rows, :], held["wqkv"][1], ones32)
    for row, bi, bj in shifted_blocks():
        if inside(bi, bj):
            qkv1[pl.ds(row, BLK), :] = qo[pl.ds(block_at(bi, bj), BLK), :]
            r1[pl.ds(row, BLK), :] = zo[pl.ds(block_at(bi, bj), BLK), :]
    for copy in copies:
        copy.wait()
    outer(o, halo_z)
    for i in range(2):
        rows = pl.ds(i * (TO // 2), TO // 2)
        qo[rows, :], _ = project(o[rows, :], held["wqkv"][1], ones32)
    for k, (row, _, _) in enumerate(outer_blocks()):
        qkv1[pl.ds(row, BLK), :] = qo[pl.ds(k * BLK, BLK), :]
    a = lax.broadcasted_iota(jnp.int32, (WT, GROUP), 0) // (2 * BLK)
    b = lax.broadcasted_iota(jnp.int32, (WT, GROUP), 1) // (2 * BLK) % 2
    apart = (a != b).astype(F32)
    lat = lax.axis_index("lat")
    top = 1.0 - apart * (lat == 0).astype(F32)
    bottom = 1.0 - apart * (lat == n_lat - 1).astype(F32)
    attend(shifted, TX // 3, qkv1, p1, scale1 * log2e, lambda n: (top, None, bottom)[n], put_o, hmask, ones64)
    for row, bi, bj in shifted_blocks():
        if inside(bi, bj):
            zo[pl.ds(block_at(bi, bj), BLK), :D] = o[pl.ds(row, BLK), :]
    hm1[...] = h1[...] + mm(zo[:, :D], held["wproj"][1]).astype(BF16).astype(F32)

    def put_second(i, rows, value):
        zo[rows, :D] = value.astype(BF16)

    feed(hm1, gain_ref[1, 1:2, :], held["wup"].at[1], held["wdown"].at[1], gp1, put_second)
    back = permutation(place_ref[...])
    fetches["whead"].wait()
    for i in range(T // ROWS):
        rows = pl.ds(i * ROWS, ROWS)
        mine = mm(back[i * ROWS : (i + 1) * ROWS], zo[:, :D]).astype(BF16)
        sb[rows, :] = (held["state"][rows, :] + mm_nt(mine, held["whead"][...])).astype(BF16)

    for name in ("w1", "w2", "rinv", "background"):
        fetches[name].wait()
    value = lax.broadcasted_iota(jnp.int32, (PV, VARS), 0) % VARS
    copies = (value == lax.broadcasted_iota(jnp.int32, (PV, VARS), 1)).astype(BF16)
    w1[...] = mm(copies, held["w1"][...].astype(BF16)).astype(BF16)
    routed(kept, recv, recv_aux, sems)
    radiance(recv, recv_aux, sb, pixel_ref[...], w1, held["w2"][...], held["rinv"][...], hot, adj)
    for i in range(T // ROWS):
        rows = pl.ds(i * ROWS, ROWS)
        value = mm(hot[rows, :], adj[...])
        gm[rows, :] = value + inverse_ref[...] * (held["state"][rows, :] - held["background"][rows, :])
        zo[rows, :D] = mm(value.astype(BF16), held["whead"][...]).astype(BF16)

    perm = permutation(order_ref[...])
    for i in range(T // ROWS):
        rows = pl.ds(i * ROWS, ROWS)
        d3 = mm(perm[i * ROWS : (i + 1) * ROWS], zo[:, :D])
        d2 = feed_back(rows, d3, hm1, gain_ref[1, 1:2, :], held["wup"].at[1], held["wdown"].at[1], gp1)
        hm1[rows, :] = d2
        put_packed(z1, i, d2.astype(BF16))
    copies = swap_edges(n_lat, n_lon, z1, halo_a, send_a, recv_a)
    wp = held["wproj"][1]
    for w in range(T // WT):
        zo[pl.ds(w * WT, WT), :D] = z1[w // 6, w % 6].reshape(WT, D)
    zo[:, D:] = mm_nt(zo[:, :D], wp).astype(BF16)
    for row, bi, bj in shifted_blocks():
        if inside(bi, bj):
            o[pl.ds(row, BLK), :] = zo[pl.ds(block_at(bi, bj), BLK), D:]
    for copy in copies:
        copy.wait()
    outer(zo.at[:, :D], halo_a)
    zo[pl.ds(0, TO), D:] = mm_nt(zo[pl.ds(0, TO), :D], wp).astype(BF16)
    for k, (row, _, _) in enumerate(outer_blocks()):
        o[pl.ds(row, BLK), :] = zo[pl.ds(k * BLK, BLK), D:]
    whole_back(
        shifted, plain, ones32, ones64, hmask, scale0, scale1, gain_ref, held, h0, hm0, h1, hm1,
        qkv0, qkv1, r0, r1, p0, p1, gp0, o, zo, qo, adj,
    )
    back = permutation(place_ref[...])
    parts = []
    for i in range(T // ROWS):
        rows = pl.ds(i * ROWS, ROWS)
        d0 = mm(back[i * ROWS : (i + 1) * ROWS], zo[:, :D]).astype(BF16)
        gm[rows, :] = gm[rows, :] + mm_nt(d0, held["wemb"][...])
        parts.append(pltpu.make_async_copy(gm.at[rows], result.at[rows], out_sem.at[i]))
        parts[-1].start()
    for part in parts:
        part.wait()


def whole_back(
    shifted, plain, ones32, ones64, hmask, scale0, scale1, gain_ref, held, h0, hm0, h1, hm1,
    qkv0, qkv1, r0, r1, p0, p1, gp0, o, zo, qo, adj,
):
    ds = adj.at[pl.ds(0, TX), pl.ds(0, 2 * GROUP)]
    dqkv = adj.at[pl.ds(TX, TX), pl.ds(0, 3 * D)]
    attend_back(shifted, TX // 3, qkv1, p1, o, ds, dqkv, scale1, hmask, ones64)
    step = TX // 3
    for i in range(3):
        rows = pl.ds(i * step, step)
        dqkv[rows, :] = through_unit(dqkv[rows, :], qkv1[rows, :], r1[rows, :], ones32)
    for row, bi, bj in shifted_blocks():
        if inside(bi, bj):
            qo[pl.ds(block_at(bi, bj), BLK), :] = dqkv[pl.ds(row, BLK), :]
    for i in range(T // ROWS):
        rows = pl.ds(i * ROWS, ROWS)
        dz = mm_nt(qo[rows, :], held["wqkv"][1])
        d1 = hm1[rows, :] + norm_back(h1[rows, :], gain_ref[1, 0:1, :], dz)
        dm = feed_back(rows, d1, hm0, gain_ref[0, 1:2, :], held["wup"].at[0], held["wdown"].at[0], gp0)
        hm1[rows, :] = dm
        o[rows, :] = mm_nt(dm.astype(BF16), held["wproj"][0]).astype(BF16)
    attend_back(plain, ROWS, qkv0, p0, o, ds, dqkv, scale0, hmask, ones64)
    for i in range(T // ROWS):
        rows = pl.ds(i * ROWS, ROWS)
        dz = mm_nt(through_unit(dqkv[rows, :], qkv0[rows, :], r0[rows, :], ones32), held["wqkv"][0])
        zo[rows, :D] = (hm1[rows, :] + norm_back(h0[rows, :], gain_ref[0, 0:1, :], dz)).astype(BF16)


def radiance(recv_ref, recv_aux_ref, moved_ref, pixel, w1_ref, w2, rinv, hot_ref, adj_ref):
    step = CHUNK
    eye = (
        lax.broadcasted_iota(jnp.int32, (16, DEV), 0) == lax.broadcasted_iota(jnp.int32, (16, DEV), 1)
    ).astype(BF16)
    lane = lax.broadcasted_iota(jnp.int32, (step, T), 1)
    row = lax.broadcasted_iota(jnp.int32, (T, step), 0)
    w2, rinv = w2.astype(BF16), rinv.astype(BF16)

    def chunk(i):
        rows = pl.ds(pl.multiple_of(i * step, step), step)
        flat16 = jnp.concatenate([recv_aux_ref[i * OWNERS + j][:, :CAP] for j in range(OWNERS)], 1)
        flat = flat16.astype(F32)
        aux = mm_tn(flat16, eye)
        live = aux[:, 3:4]
        patch = jnp.where(live > 0, aux[:, 0:1] * PIX + aux[:, 1:2], -1.0).astype(jnp.int32)
        hot = (lane == patch).astype(BF16)
        across = jnp.where(flat[3:4] > 0, flat[0:1] * PIX + flat[1:2], -1.0).astype(jnp.int32)
        hot_ref[:, rows] = (row == across).astype(BF16)
        here = pixel == aux[:, 2:3]
        found = jnp.where(here, mm(hot, moved_ref[...]), 0.0).astype(BF16)
        inner = jnp.tanh(mm(found, w1_ref[...]))
        observed = recv_ref[pl.ds(i * OWNERS, OWNERS)].reshape(step, CHAN)
        innovation = (mm(inner.astype(BF16), w2) - observed.astype(F32)) * live
        weighted = mm(innovation.astype(BF16), rinv).astype(BF16)
        pulled = mm_nt(weighted, w2) * (1.0 - inner * inner)
        adj_ref[rows, :] = jnp.where(here, mm_nt(pulled.astype(BF16), w1_ref[...]), 0.0).astype(BF16)

    def chunks(i, _):
        chunk(2 * i)
        chunk(2 * i + 1)
        return 0

    lax.fori_loop(0, SLOTS // step // 2, chunks, 0)


def whole(n_lat, n_lon, small, fetched):
    halo = [pltpu.VMEM(s + (BLK, D), BF16) for s in SHAPES]
    ANY = pl.BlockSpec(memory_space=pl.ANY)
    scratch = [pltpu.VMEM(a.shape, a.dtype) for a in fetched]
    scratch += [
        pltpu.VMEM(s, d)
        for s, d in [
            ((T, PV), BF16), ((T, D), F32), ((T, D), F32), ((T, D), F32), ((T, D), F32), (PACKED, BF16),
            ((T, 3 * D), BF16), ((TX, 3 * D), BF16), ((T, 2 * D), BF16), ((TX, 2 * D), BF16),
            ((T, 2 * GROUP), BF16), ((TX, 2 * GROUP), BF16), ((T, FFN), BF16), ((T, FFN), BF16),
            ((TX, D), BF16), ((T, 2 * D), BF16), ((T, 3 * D), BF16),
            ((T, SLOTS), BF16), ((SLOTS, PV), BF16), ((T, PV), F32),
        ]
    ]
    scratch += halo + halo
    scratch += [
        pltpu.VMEM((DEV, CAP, CHAN), BF16), pltpu.VMEM((DEV, 16, DEV), BF16), pltpu.VMEM((DEV, 16, DEV), BF16),
        pltpu.VMEM((1, OBS), jnp.int32), pltpu.VMEM((OBS, CHAN), BF16), pltpu.VMEM((PV, D), BF16),
    ]
    scratch += [pltpu.SemaphoreType.DMA((len(fetched),)), pltpu.SemaphoreType.DMA((T // ROWS,))]
    scratch += [pltpu.SemaphoreType.DMA((8,))] * 4 + [pltpu.SemaphoreType.DMA((6,))]
    return pl.pallas_call(
        functools.partial(whole_kernel, n_lat, n_lon),
        out_shape=jax.ShapeDtypeStruct((T, PV), F32),
        in_specs=[SMEM] + [VMEM] * (len(small) - 1) + [ANY] * len(fetched),
        out_specs=ANY,
        scratch_shapes=scratch,
        compiler_params=pltpu.CompilerParams(vmem_limit_bytes=62 << 20, collective_id=1, has_side_effects=True),
    )(*small, *fetched)


def local(
    n_lat, n_lon, state, background, inv_background, w_embed, norm_gain, w_qkv, w_proj, head_scale, w_up,
    w_down, w_head, w_obs1, w_obs2, r_inverse, obs_values, obs_owner, obs_point, obs_count,
):
    order = jnp.asarray(ORDER).reshape(T, 1)
    place = jnp.asarray(PLACE).reshape(T, 1)
    scales = jnp.repeat(head_scale, WT, axis=1)
    pixel = (jnp.arange(PV, dtype=jnp.int32) // VARS).astype(F32).reshape(1, PV)
    small = [
        obs_count, obs_owner.reshape(1, OBS), obs_point.reshape(1, OBS), norm_gain, scales, order, place, pixel,
        inv_background.reshape(1, PV),
    ]
    fetched = [
        obs_values, state.reshape(T, PV), w_embed, w_qkv, w_proj, w_up, w_down, w_obs1, w_obs2, r_inverse, w_head.T,
        background.reshape(T, PV),
    ]
    return whole(n_lat, n_lon, small, fetched).reshape(state.shape)


def solution(mesh):
    grid = P("lat", "lon", None)
    slots = P(("lat", "lon"))
    placed = (grid, grid) + (P(),) * 12 + (P(("lat", "lon"), None),) * 2 + (slots, slots)
    return jax.shard_map(
        functools.partial(local, mesh.shape["lat"], mesh.shape["lon"]),
        mesh=mesh,
        in_specs=placed,
        out_specs=grid,
        check_vma=False,
    )
```

```python
import functools

import jax
import jax.numpy as jnp
import numpy as np
from jax import lax
from jax.experimental import pallas as pl
from jax.experimental.pallas import tpu as pltpu
from jax.sharding import PartitionSpec as P

F32 = jnp.float32
BF16 = jnp.bfloat16
EPS = 1e-05
VARS = 69
PIX = 16
HEADS = 8
D = 256
FFN = 1024
PV = 1104
T = 768
BLK = 16
WT = 64
BR, BC = 4, 12
SW_R, SW_C = 3, 7
TX = SW_R * SW_C * WT
CAP = 32
DEV = 128
SLOTS = DEV * CAP
OBS = 2048
CHAN = 256
WIDE = 384
VMEM = pl.BlockSpec(memory_space=pltpu.VMEM)
SMEM = pl.BlockSpec(memory_space=pltpu.SMEM)


def mm(a, b):
    return jnp.dot(a, b, preferred_element_type=F32)


def mm_nt(a, b):
    return lax.dot_general(a, b, (((1,), (1,)), ((), ())), preferred_element_type=F32)


def mm_tn(a, b):
    return lax.dot_general(a, b, (((0,), (0,)), ((), ())), preferred_element_type=F32)


def block_at(bi, bj):
    return (((bi // 2) * (BC // 2) + bj // 2) * 4 + (bi % 2) * 2 + bj % 2) * BLK


def row_of_place():
    out = np.zeros((T,), np.int32)
    for bi in range(BR):
        for bj in range(BC):
            for k in range(BLK):
                out[block_at(bi, bj) + k] = (bi * 4 + k // 4) * (BC * 4) + bj * 4 + k % 4
    return out


ORDER = row_of_place()
PLACE = np.argsort(ORDER).astype(np.int32)


def permutation(column):
    return (lax.broadcasted_iota(jnp.int32, (T, T), 1) == column).astype(BF16)


def means():
    return jnp.full((D, D), 1.0 / D, BF16)


def norm_parts(x):
    high = x.astype(BF16)
    low = (x - high.astype(F32)).astype(BF16)
    centred = x - (mm(high, means()) + mm(low, means()))
    scale = lax.rsqrt(mm((centred * centred).astype(BF16), means()) + EPS)
    return centred * scale, scale


def norm(x, gain):
    return (norm_parts(x)[0] * gain).astype(BF16)


def norm_back(x, gain, dy):
    unit, scale = norm_parts(x)
    dn = dy * gain
    return scale * (dn - mm(dn.astype(BF16), means()) - unit * mm((dn * unit).astype(BF16), means()))


def same_group(n, size):
    a = lax.broadcasted_iota(jnp.int32, (n, n), 0) // size
    b = lax.broadcasted_iota(jnp.int32, (n, n), 1) // size
    return (a == b).astype(BF16)


HALF = D // 2
GROUP = 4 * WT


def head_mask():
    a = lax.broadcasted_iota(jnp.int32, (GROUP, HALF), 0) // WT
    b = lax.broadcasted_iota(jnp.int32, (GROUP, HALF), 1) // (D // HEADS)
    return (a == b).astype(BF16)


def spread(x, hmask):
    return jnp.concatenate([x] * 4, 0) * hmask


def gather_heads(x):
    lane = lax.broadcasted_iota(jnp.int32, (WT, HALF), 1) // (D // HEADS)
    out = x[:WT]
    for h in range(1, 4):
        out = jnp.where(lane == h, x[h * WT : (h + 1) * WT], out)
    return out


def project(z, wqkv, ones32):
    qkv = mm(z, wqkv).astype(BF16)
    parts, factors = [], []
    for n in range(2):
        x = qkv[:, n * D : (n + 1) * D].astype(F32)
        r = lax.rsqrt(mm((x * x).astype(BF16), ones32) + 1.0)
        parts.append((x * r).astype(BF16))
        factors.append(r.astype(BF16))
    return jnp.concatenate(parts + [qkv[:, 2 * D :]], 1), jnp.concatenate(factors, 1)


def window(w):
    return pl.ds(pl.multiple_of(w * WT, WT), WT)


def attend(groups, step, qkv_ref, p_ref, scale2, factor, put, hmask, ones64):
    length, firsts = groups

    def scores(i, _):
        for n, first in enumerate(firsts):
            rows = window(first + i)
            for g in range(2):
                lanes = pl.ds(g * HALF, HALF)
                keys = spread(qkv_ref[rows, pl.ds(D + g * HALF, HALF)], hmask)
                e = jnp.exp2(mm_nt(qkv_ref[rows, lanes], keys) * scale2[:, g * GROUP : (g + 1) * GROUP])
                f = factor(n)
                p_ref[rows, pl.ds(g * GROUP, GROUP)] = (e if f is None else e * f).astype(BF16)
        return 0

    lax.fori_loop(0, length, scores, 0)
    total = length * len(firsts) * WT
    for i in range(total // step):
        rows = pl.ds(i * step, step)
        for g in range(2):
            lanes = pl.ds(g * GROUP, GROUP)
            e = p_ref[rows, lanes]
            s = mm(e, ones64)
            p_ref[rows, lanes] = (e.astype(F32) * pl.reciprocal(s)).astype(BF16)

    def mix(i, _):
        for first in firsts:
            rows = window(first + i)
            out = []
            for g in range(2):
                values = spread(qkv_ref[rows, pl.ds(2 * D + g * HALF, HALF)], hmask)
                out.append(mm(p_ref[rows, pl.ds(g * GROUP, GROUP)], values).astype(BF16))
            put(first + i, jnp.concatenate(out, 1))
        return 0

    lax.fori_loop(0, length, mix, 0)


def attend_back(groups, step, qkv_ref, p_ref, do_ref, ds_ref, dqkv_ref, scale, hmask, ones64):
    length, firsts = groups

    def probs(i, _):
        for first in firsts:
            rows = window(first + i)
            for g in range(2):
                values = spread(qkv_ref[rows, pl.ds(2 * D + g * HALF, HALF)], hmask)
                ds_ref[rows, pl.ds(g * GROUP, GROUP)] = mm_nt(do_ref[rows, pl.ds(g * HALF, HALF)], values).astype(BF16)
        return 0

    lax.fori_loop(0, length, probs, 0)
    total = length * len(firsts) * WT
    for i in range(total // step):
        rows = pl.ds(i * step, step)
        for g in range(2):
            lanes = pl.ds(g * GROUP, GROUP)
            p = p_ref[rows, lanes].astype(F32)
            pd = p * ds_ref[rows, lanes].astype(F32)
            ds = (pd - p * mm(pd.astype(BF16), ones64)) * scale[:, g * GROUP : (g + 1) * GROUP]
            ds_ref[rows, lanes] = ds.astype(BF16)

    def rest(i, _):
        for first in firsts:
            rows = window(first + i)
            for g in range(2):
                wide, lanes = pl.ds(g * GROUP, GROUP), pl.ds(g * HALF, HALF)
                ds, p = ds_ref[rows, wide], p_ref[rows, wide]
                keys = spread(qkv_ref[rows, pl.ds(D + g * HALF, HALF)], hmask)
                dqkv_ref[rows, lanes] = mm(ds, keys).astype(BF16)
                dqkv_ref[rows, pl.ds(D + g * HALF, HALF)] = gather_heads(mm_tn(ds, qkv_ref[rows, lanes])).astype(BF16)
                dqkv_ref[rows, pl.ds(2 * D + g * HALF, HALF)] = gather_heads(mm_tn(p, do_ref[rows, lanes])).astype(BF16)
        return 0

    lax.fori_loop(0, length, rest, 0)


def through_unit(dqkv, qkv, r, ones32):
    out = []
    for n in range(2):
        lanes = slice(n * D, (n + 1) * D)
        x, dn = qkv[:, lanes].astype(F32), dqkv[:, lanes].astype(F32)
        inner = mm((x * dn).astype(BF16), ones32)
        out.append((r[:, lanes].astype(F32) * (dn - x * inner)).astype(BF16))
    return jnp.concatenate(out + [dqkv[:, 2 * D :]], 1)


ROWS = 256


def feed(hm_ref, gain, wup_ref, wdown_ref, gp_ref, put):
    for i in range(T // ROWS):
        rows = pl.ds(i * ROWS, ROWS)
        h = hm_ref[rows, :]
        u = mm(norm(h, gain), wup_ref[...])
        c = 0.7978845608028654
        square = u * u
        t = jnp.tanh(u * (c + (c * 0.044715) * square))
        half = 0.5 + 0.5 * t
        g = u * half
        gp_ref[rows, :] = (half + (g - g * half) * (2.0 * c + (6.0 * c * 0.044715) * square)).astype(BF16)
        put(i, rows, h + mm(g.astype(BF16), wdown_ref[...]))


def feed_back(rows, dh, hm_ref, gain, wup_ref, wdown_ref, gp_ref):
    dg = mm_nt(dh.astype(BF16), wdown_ref[...])
    du = (dg * gp_ref[rows, :].astype(F32)).astype(BF16)
    dn = mm_nt(du, wup_ref[...])
    return dh + norm_back(hm_ref[rows, :], gain, dn)


CHUNK = 256
OWNERS = CHUNK // CAP
HALF_OBS = OBS // 2


def other(n_lon, n):
    return (n // n_lon, lax.rem(n, n_lon))


EARLY = 4


def remote(n_lon, src, dst, n, k, sems):
    return pltpu.make_async_remote_copy(
        src_ref=src, dst_ref=dst, send_sem=sems.at[k], recv_sem=sems.at[2 + k],
        device_id=other(n_lon, n), device_id_type=pl.DeviceIdType.MESH,
    )


def turn(me, i):
    return lax.rem(i + me // OWNERS + 2 * lax.rem(me, OWNERS), DEV // OWNERS)


def send(n_lon, me, out_ref, recv, sems, i, _):
    for j in range(OWNERS):
        n = turn(me, i) * OWNERS + lax.rem(j + me, OWNERS)
        block = out_ref.at[pl.ds(pl.multiple_of(n * CAP, CAP), CAP), pl.ds(0, CHAN)]

        @pl.when(n != me)
        def _():
            remote(n_lon, block, recv.at[me], n, 0, sems).start()

    return 0


def route(n_lon, me, owner_ref, point_ref, count, values_ref, hot_ref, wide_ref, out_ref, aux_ref, recv, recv_aux, sems):
    upper = (
        lax.broadcasted_iota(jnp.int32, (CHUNK, CHUNK), 0) < lax.broadcasted_iota(jnp.int32, (CHUNK, CHUNK), 1)
    ).astype(BF16)
    carry = jnp.zeros((DEV, 1), F32)
    across = jnp.zeros((DEV, DEV), F32)
    places = []
    line = lax.broadcasted_iota(jnp.int32, (DEV, CHUNK), 0)
    kind = line // CAP
    for i in range(OBS // CHUNK):
        lanes = pl.ds(i * CHUNK, CHUNK)
        live = (lax.broadcasted_iota(jnp.int32, (1, CHUNK), 1) + i * CHUNK) < count
        owner = jnp.where(live, owner_ref[:, lanes], -1)
        hot = (line == owner).astype(F32)
        hot_ref[pl.ds(i * CHUNK // HALF_OBS * DEV, DEV), pl.ds(i * CHUNK % HALF_OBS, CHUNK)] = hot
        before = mm(hot.astype(BF16), upper) + carry
        carry = carry + jnp.sum(hot, 1, keepdims=True)
        place = jnp.sum(before * hot, 0, keepdims=True).astype(jnp.int32)
        places.append(place)
        point = point_ref[:, lanes]
        number = jnp.where(kind == 0, point // (PIX * PIX), jnp.where(kind == 1, point // PIX % PIX, point % PIX))
        number = jnp.where(line % CAP == place, jnp.where(kind < 3, number, 1), 0).astype(F32).astype(BF16)
        across = across + mm_nt(hot.astype(BF16), number)
    place = jnp.concatenate(places, 1)
    aux_ref[...] = across[:, None, :]

    def send_aux(k, _):
        n = lax.rem(me + k, DEV)
        remote(n_lon, aux_ref.at[n], recv_aux.at[me], n, 1, sems).start()
        return 0

    lax.fori_loop(1, DEV, send_aux, 0)
    wide_ref[...] = values_ref[...].astype(BF16)
    spot = (lax.broadcasted_iota(jnp.int32, (CAP, OBS), 0) == place).astype(F32)

    def chunk(i, _):
        c = turn(me, i)
        base = pl.multiple_of(c * CHUNK, CHUNK)
        mine = [hot_ref[pl.ds(pl.multiple_of(c * OWNERS + k, OWNERS), OWNERS), pl.ds(0, HALF_OBS)] for k in (0, DEV)]
        mine = jnp.concatenate(mine, 1)
        pick = jnp.concatenate([(spot * mine[j : j + 1]).astype(BF16) for j in range(OWNERS)], 0)
        out_ref[pl.ds(base, CHUNK), pl.ds(0, CHAN)] = mm(pick, wide_ref[...]).astype(BF16)
        return 0

    def chunk_sent(i, _):
        chunk(i, 0)
        return send(n_lon, me, out_ref, recv, sems, i, 0)

    lax.fori_loop(0, EARLY, chunk_sent, 0)
    lax.fori_loop(EARLY, SLOTS // CHUNK, chunk, 0)
    block = out_ref.at[pl.ds(pl.multiple_of(me * CAP, CAP), CAP), pl.ds(0, CHAN)]
    kept = [
        pltpu.make_async_copy(block, recv.at[me], sems.at[4]),
        pltpu.make_async_copy(aux_ref.at[me], recv_aux.at[me], sems.at[5]),
    ]
    for copy in kept:
        copy.start()
    return kept


def routed(kept, n, ref, sems):
    kept[n].wait()
    for k in range(2):
        part = ref.at[pl.ds(0, DEV - 1)]
        pltpu.make_async_copy(part, part, sems.at[2 * k + n]).wait()


SIDES = [(-1, 0), (1, 0), (0, -1), (0, 1), (-1, -1), (-1, 1), (1, -1), (1, 1)]
SHAPES = [(6, 2), (6, 2), (2, 2), (2, 2), (), (), (), ()]
PACKED = (2, 6, 2, 2, BLK, D)


def edge(ref, side):
    r, c = side
    i, j = (0 if r < 0 else 1), (0 if c < 0 else 1)
    if c == 0:
        return ref.at[i, :, i]
    if r == 0:
        return ref.at[:, 5 * j, :, j]
    return ref.at[i, 5 * j, i, j]


def put_packed(ref, i, value):
    for k in range(ROWS // WT):
        w = i * (ROWS // WT) + k
        ref[w // 6, w % 6] = value[k * WT : (k + 1) * WT].reshape(2, 2, BLK, D)


def neighbour(n_lat, n_lon, side):
    lat, lon = lax.axis_index("lat"), lax.axis_index("lon")
    return (lax.rem(lat + side[0] + n_lat, n_lat), lax.rem(lon + side[1] + n_lon, n_lon))


def swap_edges(n_lat, n_lon, z_ref, halos, send, recv):
    copies = []
    for n, side in enumerate(SIDES):
        opposite = SIDES.index((-side[0], -side[1]))
        copies.append(
            pltpu.make_async_remote_copy(
                src_ref=edge(z_ref, side),
                dst_ref=halos[opposite],
                send_sem=send.at[n],
                recv_sem=recv.at[opposite],
                device_id=neighbour(n_lat, n_lon, side),
                device_id_type=pl.DeviceIdType.MESH,
            )
        )
        copies[-1].start()
    return copies


def shifted_blocks():
    for si in range(SW_R):
        for sj in range(SW_C):
            for k in range(4):
                yield ((si * SW_C + sj) * 4 + k) * BLK, 2 * si - 1 + k // 2, 2 * sj - 1 + k % 2


def inside(bi, bj):
    return 0 <= bi < BR and 0 <= bj < BC


def outer(out_ref, halos):
    for n, (_, bi, bj) in enumerate(outer_blocks()):
        r = -1 if bi < 0 else 1 if bi >= BR else 0
        c = -1 if bj < 0 else 1 if bj >= BC else 0
        halo = halos[SIDES.index((r, c))]
        if c == 0:
            value = halo[bj // 2, bj % 2]
        elif r == 0:
            value = halo[bi // 2, bi % 2]
        else:
            value = halo[...]
        out_ref[pl.ds(n * BLK, BLK), :] = value


def outer_blocks():
    return [b for b in shifted_blocks() if not inside(b[1], b[2])]


TO = len(outer_blocks()) * BLK


FETCHED = ["values", "state", "wemb", "wqkv", "wproj", "wup", "wdown", "w1", "w2", "rinv", "whead", "background"]


def whole_kernel(
    n_lat, n_lon, count_ref, owner_ref, point_ref, gain_ref, scale_ref, order_ref, place_ref, pixel_ref, inverse_ref,
    *refs,
):
    n = len(FETCHED)
    source = dict(zip(FETCHED, refs[:n]))
    result = refs[n]
    refs = refs[n + 1 :]
    held = dict(zip(FETCHED, refs[: n - 1]))
    refs = refs[n - 1 :]
    n = 0
    (sb, h0, hm0, h1, hm1, z1, qkv0, qkv1, r0, r1, p0, p1, gp0, gp1, o, zo, qo, hot, adj, gm) = refs[n : n + 20]
    held["background"] = gm
    halo_z, halo_a = refs[n + 20 : n + 28], refs[n + 28 : n + 36]
    recv, recv_aux, send_aux, w1, fetch_sem, out_sem, send_z, recv_z, send_a, recv_a, sems = refs[n + 36 :]
    fetches = {name: pltpu.make_async_copy(source[name], held[name], fetch_sem.at[k]) for k, name in enumerate(FETCHED)}
    for name in FETCHED[:-1]:
        fetches[name].start()
    barrier = pltpu.get_barrier_semaphore()
    me = lax.axis_index("lat") * n_lon + lax.axis_index("lon")

    def greet(k, _):
        pl.semaphore_signal(
            barrier, inc=1, device_id=other(n_lon, lax.rem(me + k, DEV)), device_id_type=pl.DeviceIdType.MESH
        )
        return 0

    lax.fori_loop(1, DEV, greet, 0)
    ones32, ones64, hmask = same_group(D, D // HEADS), same_group(GROUP, WT), head_mask()
    log2e = 1.4426950408889634
    scale0, scale1 = scale_ref[0:1, :], scale_ref[1:2, :]
    plain = (1, list(range(T // WT)))
    shifted = (1, list(range(TX // WT)))

    fetches["values"].wait()
    pl.semaphore_wait(barrier, DEV - 1)
    kept = route(
        n_lon, me, owner_ref, point_ref, count_ref[0], held["values"], gm,
        adj.at[pl.ds(0, OBS), pl.ds(CHAN, CHAN)], adj, send_aux, recv, recv_aux, sems,
    )

    fetches["background"].start()

    perm = permutation(order_ref[...])
    fetches["state"].wait()
    sb[...] = held["state"][...].astype(BF16)
    fetches["wemb"].wait()
    fetches["wqkv"].wait()
    for i in range(T // ROWS):
        rows = pl.ds(i * ROWS, ROWS)
        mine = mm(perm[i * ROWS : (i + 1) * ROWS], sb[...]).astype(BF16)
        hidden = mm(mine, held["wemb"][...])
        h0[rows, :] = hidden
        qkv0[rows, :], r0[rows, :] = project(norm(hidden, gain_ref[0, 0:1, :]), held["wqkv"][0], ones32)

    def put_o(w, value):
        o[window(w), :] = value

    attend(plain, ROWS, qkv0, p0, scale0 * log2e, lambda n: None, put_o, hmask, ones64)
    fetches["wproj"].wait()
    fetches["wup"].wait()
    fetches["wdown"].wait()
    hm0[...] = h0[...] + mm(o[pl.ds(0, T), :], held["wproj"][0]).astype(BF16).astype(F32)

    def put_first(i, rows, value):
        h1[rows, :] = value
        put_packed(z1, i, norm(value, gain_ref[1, 0:1, :]))

    feed(hm0, gain_ref[0, 1:2, :], held["wup"].at[0], held["wdown"].at[0], gp0, put_first)

    copies = swap_edges(n_lat, n_lon, z1, halo_z, send_z, recv_z)
    lax.fori_loop(EARLY, SLOTS // CHUNK, functools.partial(send, n_lon, me, adj, recv, sems), 0)
    for i in range(T // ROWS):
        for k in range(ROWS // WT):
            w = i * (ROWS // WT) + k
            o[pl.ds(w * WT, WT), :] = z1[w // 6, w % 6].reshape(WT, D)
        rows = pl.ds(i * ROWS, ROWS)
        qo[rows, :], zo[rows, :] = project(o[rows, :], held["wqkv"][1], ones32)
    for row, bi, bj in shifted_blocks():
        if inside(bi, bj):
            qkv1[pl.ds(row, BLK), :] = qo[pl.ds(block_at(bi, bj), BLK), :]
            r1[pl.ds(row, BLK), :] = zo[pl.ds(block_at(bi, bj), BLK), :]
    for copy in copies:
        copy.wait()
    outer(o, halo_z)
    for i in range(2):
        rows = pl.ds(i * (TO // 2), TO // 2)
        qo[rows, :], _ = project(o[rows, :], held["wqkv"][1], ones32)
    for k, (row, _, _) in enumerate(outer_blocks()):
        qkv1[pl.ds(row, BLK), :] = qo[pl.ds(k * BLK, BLK), :]
    a = lax.broadcasted_iota(jnp.int32, (WT, GROUP), 0) // (2 * BLK)
    b = lax.broadcasted_iota(jnp.int32, (WT, GROUP), 1) // (2 * BLK) % 2
    apart = (a != b).astype(F32)
    lat = lax.axis_index("lat")
    top = 1.0 - apart * (lat == 0).astype(F32)
    bottom = 1.0 - apart * (lat == n_lat - 1).astype(F32)
    attend(shifted, TX // 3, qkv1, p1, scale1 * log2e, lambda n: (top, None, bottom)[n // SW_C], put_o, hmask, ones64)
    for row, bi, bj in shifted_blocks():
        if inside(bi, bj):
            zo[pl.ds(block_at(bi, bj), BLK), :D] = o[pl.ds(row, BLK), :]
    hm1[...] = h1[...] + mm(zo[:, :D], held["wproj"][1]).astype(BF16).astype(F32)

    def put_second(i, rows, value):
        zo[rows, :D] = value.astype(BF16)

    feed(hm1, gain_ref[1, 1:2, :], held["wup"].at[1], held["wdown"].at[1], gp1, put_second)
    back = permutation(place_ref[...])
    fetches["whead"].wait()
    for i in range(T // ROWS):
        rows = pl.ds(i * ROWS, ROWS)
        mine = mm(back[i * ROWS : (i + 1) * ROWS], zo[:, :D]).astype(BF16)
        sb[rows, :] = (held["state"][rows, :] + mm_nt(mine, held["whead"][...])).astype(BF16)

    for name in ("w1", "w2", "rinv", "background"):
        fetches[name].wait()
    value = lax.broadcasted_iota(jnp.int32, (PV, VARS), 0) % VARS
    copies = (value == lax.broadcasted_iota(jnp.int32, (PV, VARS), 1)).astype(BF16)
    w1[...] = mm(copies, held["w1"][...].astype(BF16)).astype(BF16)
    routed(kept, 1, recv_aux, sems)
    inner = adj.at[pl.ds(0, SLOTS), pl.ds(CHAN, CHAN)]
    numbers = recv_aux[:, 0, :].astype(BF16)
    radiance(numbers, sb, pixel_ref[...], w1, hot, inner)
    routed(kept, 0, recv, sems)
    radiance_back(numbers, recv, pixel_ref[...], w1, held["w2"][...], held["rinv"][...], inner, adj)
    for i in range(T // ROWS):
        rows = pl.ds(i * ROWS, ROWS)
        value = mm(hot[rows, :], adj[...])
        gm[rows, :] = value + inverse_ref[...] * (held["state"][rows, :] - held["background"][rows, :])
        zo[rows, :D] = mm(value.astype(BF16), held["whead"][...]).astype(BF16)

    perm = permutation(order_ref[...])
    for i in range(T // ROWS):
        rows = pl.ds(i * ROWS, ROWS)
        d3 = mm(perm[i * ROWS : (i + 1) * ROWS], zo[:, :D])
        d2 = feed_back(rows, d3, hm1, gain_ref[1, 1:2, :], held["wup"].at[1], held["wdown"].at[1], gp1)
        hm1[rows, :] = d2
        put_packed(z1, i, d2.astype(BF16))
    copies = swap_edges(n_lat, n_lon, z1, halo_a, send_a, recv_a)
    wp = held["wproj"][1]
    for w in range(T // WT):
        zo[pl.ds(w * WT, WT), :D] = z1[w // 6, w % 6].reshape(WT, D)
    zo[:, D:] = mm_nt(zo[:, :D], wp).astype(BF16)
    for row, bi, bj in shifted_blocks():
        if inside(bi, bj):
            o[pl.ds(row, BLK), :] = zo[pl.ds(block_at(bi, bj), BLK), D:]
    for copy in copies:
        copy.wait()
    outer(zo.at[:, :D], halo_a)
    zo[pl.ds(0, TO), D:] = mm_nt(zo[pl.ds(0, TO), :D], wp).astype(BF16)
    for k, (row, _, _) in enumerate(outer_blocks()):
        o[pl.ds(row, BLK), :] = zo[pl.ds(k * BLK, BLK), D:]
    whole_back(
        shifted, plain, ones32, ones64, hmask, scale0, scale1, gain_ref, held, h0, hm0, h1, hm1,
        qkv0, qkv1, r0, r1, p0, p1, gp0, o, zo, qo, adj,
    )
    back = permutation(place_ref[...])
    parts = []
    for i in range(T // ROWS):
        rows = pl.ds(i * ROWS, ROWS)
        d0 = mm(back[i * ROWS : (i + 1) * ROWS], zo[:, :D]).astype(BF16)
        gm[rows, :] = gm[rows, :] + mm_nt(d0, held["wemb"][...])
        parts.append(pltpu.make_async_copy(gm.at[rows], result.at[rows], out_sem.at[i]))
        parts[-1].start()
    for part in parts:
        part.wait()


def whole_back(
    shifted, plain, ones32, ones64, hmask, scale0, scale1, gain_ref, held, h0, hm0, h1, hm1,
    qkv0, qkv1, r0, r1, p0, p1, gp0, o, zo, qo, adj,
):
    ds = adj.at[pl.ds(0, TX), pl.ds(0, 2 * GROUP)]
    dqkv = adj.at[pl.ds(TX, TX), pl.ds(0, 3 * D)]
    attend_back(shifted, TX // 3, qkv1, p1, o, ds, dqkv, scale1, hmask, ones64)
    step = TX // 3
    for i in range(3):
        rows = pl.ds(i * step, step)
        dqkv[rows, :] = through_unit(dqkv[rows, :], qkv1[rows, :], r1[rows, :], ones32)
    for row, bi, bj in shifted_blocks():
        if inside(bi, bj):
            qo[pl.ds(block_at(bi, bj), BLK), :] = dqkv[pl.ds(row, BLK), :]
    for i in range(T // ROWS):
        rows = pl.ds(i * ROWS, ROWS)
        dz = mm_nt(qo[rows, :], held["wqkv"][1])
        d1 = hm1[rows, :] + norm_back(h1[rows, :], gain_ref[1, 0:1, :], dz)
        dm = feed_back(rows, d1, hm0, gain_ref[0, 1:2, :], held["wup"].at[0], held["wdown"].at[0], gp0)
        hm1[rows, :] = dm
        o[rows, :] = mm_nt(dm.astype(BF16), held["wproj"][0]).astype(BF16)
    attend_back(plain, ROWS, qkv0, p0, o, ds, dqkv, scale0, hmask, ones64)
    for i in range(T // ROWS):
        rows = pl.ds(i * ROWS, ROWS)
        dz = mm_nt(through_unit(dqkv[rows, :], qkv0[rows, :], r0[rows, :], ones32), held["wqkv"][0])
        zo[rows, :D] = (hm1[rows, :] + norm_back(h0[rows, :], gain_ref[0, 0:1, :], dz)).astype(BF16)


STEP = 512


def numbers_of(numbers, i):
    slot = lax.broadcasted_iota(jnp.int32, (STEP, DEV), 0)
    across = lax.broadcasted_iota(jnp.int32, (STEP, DEV), 1)
    kinds = (
        lax.broadcasted_iota(jnp.int32, (DEV, DEV), 0) // CAP == lax.broadcasted_iota(jnp.int32, (DEV, DEV), 1)
    ).astype(BF16)
    sender = (slot // CAP + i * (STEP // CAP) == across).astype(BF16)
    mine = jnp.where(across % CAP == slot % CAP, mm(sender, numbers), 0.0)
    return mm(mine.astype(BF16), kinds)


def in_pairs(chunk):
    def chunks(i, _):
        chunk(2 * i)
        chunk(2 * i + 1)
        return 0

    lax.fori_loop(0, SLOTS // STEP // 2, chunks, 0)


def radiance(numbers, moved_ref, pixel, w1_ref, hot_ref, inner_ref):
    eye = (
        lax.broadcasted_iota(jnp.int32, (16, DEV), 0) == lax.broadcasted_iota(jnp.int32, (16, DEV), 1)
    ).astype(BF16)
    lane = lax.broadcasted_iota(jnp.int32, (STEP, T), 1)
    row = lax.broadcasted_iota(jnp.int32, (T, STEP), 0)

    def chunk(i):
        rows = pl.ds(pl.multiple_of(i * STEP, STEP), STEP)
        aux = numbers_of(numbers, i)
        flat = mm_nt(eye, aux.astype(BF16))
        patch = jnp.where(aux[:, 3:4] > 0, aux[:, 0:1] * PIX + aux[:, 1:2], -1.0).astype(jnp.int32)
        hot = (lane == patch).astype(BF16)
        patches = jnp.where(flat[3:4] > 0, flat[0:1] * PIX + flat[1:2], -1.0).astype(jnp.int32)
        hot_ref[:, rows] = (row == patches).astype(BF16)
        found = jnp.where(pixel == aux[:, 2:3], mm(hot, moved_ref[...]), 0.0).astype(BF16)
        inner_ref[rows, :] = jnp.tanh(mm(found, w1_ref[...])).astype(BF16)

    in_pairs(chunk)


def radiance_back(numbers, recv_ref, pixel, w1_ref, w2, rinv, inner_ref, adj_ref):
    w2, rinv = w2.astype(BF16), rinv.astype(BF16)

    def chunk(i):
        rows = pl.ds(pl.multiple_of(i * STEP, STEP), STEP)
        aux = numbers_of(numbers, i)
        inner16 = inner_ref[rows, :]
        inner = inner16.astype(F32)
        observed = recv_ref[pl.ds(i * (STEP // CAP), STEP // CAP)].reshape(STEP, CHAN)
        innovation = (mm(inner16, w2) - observed.astype(F32)) * aux[:, 3:4]
        weighted = mm(innovation.astype(BF16), rinv).astype(BF16)
        pulled = mm_nt(weighted, w2) * (1.0 - inner * inner)
        adj = mm_nt(pulled.astype(BF16), w1_ref[...])
        adj_ref[rows, :] = jnp.where(pixel == aux[:, 2:3], adj, 0.0).astype(BF16)

    in_pairs(chunk)


def whole(n_lat, n_lon, small, fetched):
    halo = [pltpu.VMEM(s + (BLK, D), BF16) for s in SHAPES]
    ANY = pl.BlockSpec(memory_space=pl.ANY)
    scratch = [pltpu.VMEM(a.shape, a.dtype) for a in fetched[:-1]]
    scratch += [
        pltpu.VMEM(s, d)
        for s, d in [
            ((T, PV), BF16), ((T, D), F32), ((T, D), F32), ((T, D), F32), ((T, D), F32), (PACKED, BF16),
            ((T, 3 * D), BF16), ((TX, 3 * D), BF16), ((T, 2 * D), BF16), ((TX, 2 * D), BF16),
            ((T, 2 * GROUP), BF16), ((TX, 2 * GROUP), BF16), ((T, FFN), BF16), ((T, FFN), BF16),
            ((TX, D), BF16), ((T, 2 * D), BF16), ((T, 3 * D), BF16),
            ((T, SLOTS), BF16), ((SLOTS, PV), BF16), ((T, PV), F32),
        ]
    ]
    scratch += halo + halo
    scratch += [
        pltpu.VMEM((DEV, CAP, CHAN), BF16), pltpu.VMEM((DEV, 1, DEV), F32), pltpu.VMEM((DEV, 1, DEV), F32),
        pltpu.VMEM((PV, D), BF16),
    ]
    scratch += [pltpu.SemaphoreType.DMA((len(fetched),)), pltpu.SemaphoreType.DMA((T // ROWS,))]
    scratch += [pltpu.SemaphoreType.DMA((8,))] * 4 + [pltpu.SemaphoreType.DMA((6,))]
    return pl.pallas_call(
        functools.partial(whole_kernel, n_lat, n_lon),
        out_shape=jax.ShapeDtypeStruct((T, PV), F32),
        in_specs=[SMEM] + [VMEM] * (len(small) - 1) + [ANY] * len(fetched),
        out_specs=ANY,
        scratch_shapes=scratch,
        compiler_params=pltpu.CompilerParams(vmem_limit_bytes=62 << 20, collective_id=1, has_side_effects=True),
    )(*small, *fetched)


def local(
    n_lat, n_lon, state, background, inv_background, w_embed, norm_gain, w_qkv, w_proj, head_scale, w_up,
    w_down, w_head, w_obs1, w_obs2, r_inverse, obs_values, obs_owner, obs_point, obs_count,
):
    order = jnp.asarray(ORDER).reshape(T, 1)
    place = jnp.asarray(PLACE).reshape(T, 1)
    scales = jnp.repeat(head_scale, WT, axis=1)
    pixel = (jnp.arange(PV, dtype=jnp.int32) // VARS).astype(F32).reshape(1, PV)
    small = [
        obs_count, obs_owner.reshape(1, OBS), obs_point.reshape(1, OBS), norm_gain, scales, order, place, pixel,
        inv_background.reshape(1, PV),
    ]
    fetched = [
        obs_values, state.reshape(T, PV), w_embed, w_qkv, w_proj, w_up, w_down, w_obs1, w_obs2, r_inverse, w_head.T,
        background.reshape(T, PV),
    ]
    return whole(n_lat, n_lon, small, fetched).reshape(state.shape)


def solution(mesh):
    grid = P("lat", "lon", None)
    slots = P(("lat", "lon"))
    placed = (grid, grid) + (P(),) * 12 + (P(("lat", "lon"), None),) * 2 + (slots, slots)
    return jax.shard_map(
        functools.partial(local, mesh.shape["lat"], mesh.shape["lon"]),
        mesh=mesh,
        in_specs=placed,
        out_specs=grid,
        check_vma=False,
    )
```

```python
import functools

import jax
import jax.numpy as jnp
import numpy as np
from jax import lax
from jax.experimental import pallas as pl
from jax.experimental.pallas import tpu as pltpu
from jax.sharding import PartitionSpec as P

F32 = jnp.float32
BF16 = jnp.bfloat16
EPS = 1e-05
VARS = 69
PIX = 16
HEADS = 8
D = 256
FFN = 1024
PV = 1104
T = 768
BLK = 16
WT = 64
BR, BC = 4, 12
SW_R, SW_C = 3, 7
TX = SW_R * SW_C * WT
CAP = 32
DEV = 128
SLOTS = DEV * CAP
OBS = 2048
CHAN = 256
WIDE = 384
VMEM = pl.BlockSpec(memory_space=pltpu.VMEM)
SMEM = pl.BlockSpec(memory_space=pltpu.SMEM)


def mm(a, b):
    return jnp.dot(a, b, preferred_element_type=F32)


def mm_nt(a, b):
    return lax.dot_general(a, b, (((1,), (1,)), ((), ())), preferred_element_type=F32)


def mm_tn(a, b):
    return lax.dot_general(a, b, (((0,), (0,)), ((), ())), preferred_element_type=F32)


def block_at(bi, bj):
    return (((bi // 2) * (BC // 2) + bj // 2) * 4 + (bi % 2) * 2 + bj % 2) * BLK


def row_of_place():
    out = np.zeros((T,), np.int32)
    for bi in range(BR):
        for bj in range(BC):
            for k in range(BLK):
                out[block_at(bi, bj) + k] = (bi * 4 + k // 4) * (BC * 4) + bj * 4 + k % 4
    return out


ORDER = row_of_place()
PLACE = np.argsort(ORDER).astype(np.int32)


def permutation(column):
    return (lax.broadcasted_iota(jnp.int32, (T, T), 1) == column).astype(BF16)


def means():
    return jnp.full((D, D), 1.0 / D, BF16)


def norm_parts(x):
    high = x.astype(BF16)
    low = (x - high.astype(F32)).astype(BF16)
    centred = x - (mm(high, means()) + mm(low, means()))
    scale = lax.rsqrt(mm((centred * centred).astype(BF16), means()) + EPS)
    return centred * scale, scale


def norm(x, gain):
    return (norm_parts(x)[0] * gain).astype(BF16)


def norm_back(x, gain, dy):
    unit, scale = norm_parts(x)
    dn = dy * gain
    return scale * (dn - mm(dn.astype(BF16), means()) - unit * mm((dn * unit).astype(BF16), means()))


def same_group(n, size):
    a = lax.broadcasted_iota(jnp.int32, (n, n), 0) // size
    b = lax.broadcasted_iota(jnp.int32, (n, n), 1) // size
    return (a == b).astype(BF16)


HALF = D // 2
GROUP = 4 * WT


def head_mask():
    a = lax.broadcasted_iota(jnp.int32, (GROUP, HALF), 0) // WT
    b = lax.broadcasted_iota(jnp.int32, (GROUP, HALF), 1) // (D // HEADS)
    return (a == b).astype(BF16)


def spread(x, hmask):
    return jnp.concatenate([x] * 4, 0) * hmask


def gather_heads(x):
    lane = lax.broadcasted_iota(jnp.int32, (WT, HALF), 1) // (D // HEADS)
    out = x[:WT]
    for h in range(1, 4):
        out = jnp.where(lane == h, x[h * WT : (h + 1) * WT], out)
    return out


def project(z, wqkv, ones32):
    qkv = mm(z, wqkv).astype(BF16)
    parts, factors = [], []
    for n in range(2):
        x = qkv[:, n * D : (n + 1) * D].astype(F32)
        r = lax.rsqrt(mm((x * x).astype(BF16), ones32) + 1.0)
        parts.append((x * r).astype(BF16))
        factors.append(r.astype(BF16))
    return jnp.concatenate(parts + [qkv[:, 2 * D :]], 1), jnp.concatenate(factors, 1)


def window(w):
    return pl.ds(pl.multiple_of(w * WT, WT), WT)


def attend(groups, step, qkv_ref, p_ref, scale2, factor, put, hmask, ones64):
    length, firsts = groups

    def scores(i, _):
        for n, first in enumerate(firsts):
            rows = window(first + i)
            for g in range(2):
                lanes = pl.ds(g * HALF, HALF)
                keys = spread(qkv_ref[rows, pl.ds(D + g * HALF, HALF)], hmask)
                e = jnp.exp2(mm_nt(qkv_ref[rows, lanes], keys) * scale2[:, g * GROUP : (g + 1) * GROUP])
                f = factor(n)
                p_ref[rows, pl.ds(g * GROUP, GROUP)] = (e if f is None else e * f).astype(BF16)
        return 0

    lax.fori_loop(0, length, scores, 0)
    total = length * len(firsts) * WT
    for i in range(total // step):
        rows = pl.ds(i * step, step)
        for g in range(2):
            lanes = pl.ds(g * GROUP, GROUP)
            e = p_ref[rows, lanes]
            s = mm(e, ones64)
            p_ref[rows, lanes] = (e.astype(F32) * pl.reciprocal(s)).astype(BF16)

    def mix(i, _):
        for first in firsts:
            rows = window(first + i)
            out = []
            for g in range(2):
                values = spread(qkv_ref[rows, pl.ds(2 * D + g * HALF, HALF)], hmask)
                out.append(mm(p_ref[rows, pl.ds(g * GROUP, GROUP)], values).astype(BF16))
            put(first + i, jnp.concatenate(out, 1))
        return 0

    lax.fori_loop(0, length, mix, 0)


def attend_back(groups, step, qkv_ref, p_ref, do_ref, ds_ref, dqkv_ref, scale, hmask, ones64):
    length, firsts = groups

    def probs(i, _):
        for first in firsts:
            rows = window(first + i)
            for g in range(2):
                values = spread(qkv_ref[rows, pl.ds(2 * D + g * HALF, HALF)], hmask)
                ds_ref[rows, pl.ds(g * GROUP, GROUP)] = mm_nt(do_ref[rows, pl.ds(g * HALF, HALF)], values).astype(BF16)
        return 0

    lax.fori_loop(0, length, probs, 0)
    total = length * len(firsts) * WT
    for i in range(total // step):
        rows = pl.ds(i * step, step)
        for g in range(2):
            lanes = pl.ds(g * GROUP, GROUP)
            p = p_ref[rows, lanes].astype(F32)
            pd = p * ds_ref[rows, lanes].astype(F32)
            ds = (pd - p * mm(pd.astype(BF16), ones64)) * scale[:, g * GROUP : (g + 1) * GROUP]
            ds_ref[rows, lanes] = ds.astype(BF16)

    def rest(i, _):
        for first in firsts:
            rows = window(first + i)
            for g in range(2):
                wide, lanes = pl.ds(g * GROUP, GROUP), pl.ds(g * HALF, HALF)
                ds, p = ds_ref[rows, wide], p_ref[rows, wide]
                keys = spread(qkv_ref[rows, pl.ds(D + g * HALF, HALF)], hmask)
                dqkv_ref[rows, lanes] = mm(ds, keys).astype(BF16)
                dqkv_ref[rows, pl.ds(D + g * HALF, HALF)] = gather_heads(mm_tn(ds, qkv_ref[rows, lanes])).astype(BF16)
                dqkv_ref[rows, pl.ds(2 * D + g * HALF, HALF)] = gather_heads(mm_tn(p, do_ref[rows, lanes])).astype(BF16)
        return 0

    lax.fori_loop(0, length, rest, 0)


def through_unit(dqkv, qkv, r, ones32):
    out = []
    for n in range(2):
        lanes = slice(n * D, (n + 1) * D)
        x, dn = qkv[:, lanes].astype(F32), dqkv[:, lanes].astype(F32)
        inner = mm((x * dn).astype(BF16), ones32)
        out.append((r[:, lanes].astype(F32) * (dn - x * inner)).astype(BF16))
    return jnp.concatenate(out + [dqkv[:, 2 * D :]], 1)


ROWS = 256


def feed(hm_ref, gain, wup_ref, wdown_ref, gp_ref, put):
    for i in range(T // ROWS):
        rows = pl.ds(i * ROWS, ROWS)
        h = hm_ref[rows, :]
        u = mm(norm(h, gain), wup_ref[...])
        c = 0.7978845608028654
        square = u * u
        t = jnp.tanh(u * (c + (c * 0.044715) * square))
        half = 0.5 + 0.5 * t
        g = u * half
        gp_ref[rows, :] = (half + (g - g * half) * (2.0 * c + (6.0 * c * 0.044715) * square)).astype(BF16)
        put(i, rows, h + mm(g.astype(BF16), wdown_ref[...]))


def feed_back(rows, dh, hm_ref, gain, wup_ref, wdown_ref, gp_ref):
    dg = mm_nt(dh.astype(BF16), wdown_ref[...])
    du = (dg * gp_ref[rows, :].astype(F32)).astype(BF16)
    dn = mm_nt(du, wup_ref[...])
    return dh + norm_back(hm_ref[rows, :], gain, dn)


CHUNK = 256
OWNERS = CHUNK // CAP
HALF_OBS = OBS // 2


def other(n_lon, n):
    return (n // n_lon, lax.rem(n, n_lon))


EARLY = 12


def remote(n_lon, src, dst, n, k, sems):
    return pltpu.make_async_remote_copy(
        src_ref=src, dst_ref=dst, send_sem=sems.at[k], recv_sem=sems.at[2 + k],
        device_id=other(n_lon, n), device_id_type=pl.DeviceIdType.MESH,
    )


def turn(me, i):
    return lax.rem(i + me // OWNERS + 2 * lax.rem(me, OWNERS), DEV // OWNERS)


def send(n_lon, me, out_ref, recv, sems, i, _):
    for j in range(OWNERS):
        n = turn(me, i) * OWNERS + lax.rem(j + me, OWNERS)
        block = out_ref.at[pl.ds(pl.multiple_of(n * CAP, CAP), CAP), pl.ds(0, CHAN)]

        @pl.when(n != me)
        def _():
            remote(n_lon, block, recv.at[me], n, 0, sems).start()

    return 0


def route(n_lon, me, owner_ref, point_ref, count, values_ref, hot_ref, wide_ref, out_ref, aux_ref, recv, recv_aux, sems):
    upper = (
        lax.broadcasted_iota(jnp.int32, (CHUNK, CHUNK), 0) < lax.broadcasted_iota(jnp.int32, (CHUNK, CHUNK), 1)
    ).astype(BF16)
    carry = jnp.zeros((DEV, 1), F32)
    across = jnp.zeros((DEV, DEV), F32)
    places = []
    line = lax.broadcasted_iota(jnp.int32, (DEV, CHUNK), 0)
    kind = line // CAP
    for i in range(OBS // CHUNK):
        lanes = pl.ds(i * CHUNK, CHUNK)
        live = (lax.broadcasted_iota(jnp.int32, (1, CHUNK), 1) + i * CHUNK) < count
        owner = jnp.where(live, owner_ref[:, lanes], -1)
        hot = (line == owner).astype(F32)
        hot_ref[pl.ds(i * CHUNK // HALF_OBS * DEV, DEV), pl.ds(i * CHUNK % HALF_OBS, CHUNK)] = hot
        before = mm(hot.astype(BF16), upper) + carry
        carry = carry + jnp.sum(hot, 1, keepdims=True)
        place = jnp.sum(before * hot, 0, keepdims=True).astype(jnp.int32)
        places.append(place)
        point = point_ref[:, lanes]
        number = jnp.where(kind == 0, point // (PIX * PIX), jnp.where(kind == 1, point // PIX % PIX, point % PIX))
        number = jnp.where(line % CAP == place, jnp.where(kind < 3, number, 1), 0).astype(F32).astype(BF16)
        across = across + mm_nt(hot.astype(BF16), number)
    place = jnp.concatenate(places, 1)
    aux_ref[...] = across[:, None, :]

    def send_aux(k, _):
        n = lax.rem(me + k, DEV)
        remote(n_lon, aux_ref.at[n], recv_aux.at[me], n, 1, sems).start()
        return 0

    lax.fori_loop(1, DEV, send_aux, 0)
    wide_ref[...] = values_ref[...].astype(BF16)
    spot = (lax.broadcasted_iota(jnp.int32, (CAP, OBS), 0) == place).astype(F32)

    def chunk(i, _):
        c = turn(me, i)
        base = pl.multiple_of(c * CHUNK, CHUNK)
        mine = [hot_ref[pl.ds(pl.multiple_of(c * OWNERS + k, OWNERS), OWNERS), pl.ds(0, HALF_OBS)] for k in (0, DEV)]
        mine = jnp.concatenate(mine, 1)
        pick = jnp.concatenate([(spot * mine[j : j + 1]).astype(BF16) for j in range(OWNERS)], 0)
        out_ref[pl.ds(base, CHUNK), pl.ds(0, CHAN)] = mm(pick, wide_ref[...]).astype(BF16)
        return 0

    def chunk_sent(i, _):
        chunk(i, 0)
        return send(n_lon, me, out_ref, recv, sems, i, 0)

    lax.fori_loop(0, EARLY, chunk_sent, 0)
    lax.fori_loop(EARLY, SLOTS // CHUNK, chunk, 0)
    block = out_ref.at[pl.ds(pl.multiple_of(me * CAP, CAP), CAP), pl.ds(0, CHAN)]
    kept = [
        pltpu.make_async_copy(block, recv.at[me], sems.at[4]),
        pltpu.make_async_copy(aux_ref.at[me], recv_aux.at[me], sems.at[5]),
    ]
    for copy in kept:
        copy.start()
    return kept


def routed(kept, n, ref, sems):
    kept[n].wait()
    for k in range(2):
        part = ref.at[pl.ds(0, DEV - 1)]
        pltpu.make_async_copy(part, part, sems.at[2 * k + n]).wait()


SIDES = [(-1, 0), (1, 0), (0, -1), (0, 1), (-1, -1), (-1, 1), (1, -1), (1, 1)]
SHAPES = [(6, 2), (6, 2), (2, 2), (2, 2), (), (), (), ()]
PACKED = (2, 6, 2, 2, BLK, D)


def edge(ref, side):
    r, c = side
    i, j = (0 if r < 0 else 1), (0 if c < 0 else 1)
    if c == 0:
        return ref.at[i, :, i]
    if r == 0:
        return ref.at[:, 5 * j, :, j]
    return ref.at[i, 5 * j, i, j]


def put_packed(ref, i, value):
    for k in range(ROWS // WT):
        w = i * (ROWS // WT) + k
        ref[w // 6, w % 6] = value[k * WT : (k + 1) * WT].reshape(2, 2, BLK, D)


def neighbour(n_lat, n_lon, side):
    lat, lon = lax.axis_index("lat"), lax.axis_index("lon")
    return (lax.rem(lat + side[0] + n_lat, n_lat), lax.rem(lon + side[1] + n_lon, n_lon))


def swap_edges(n_lat, n_lon, z_ref, halos, send, recv):
    copies = []
    for n, side in enumerate(SIDES):
        opposite = SIDES.index((-side[0], -side[1]))
        copies.append(
            pltpu.make_async_remote_copy(
                src_ref=edge(z_ref, side),
                dst_ref=halos[opposite],
                send_sem=send.at[n],
                recv_sem=recv.at[opposite],
                device_id=neighbour(n_lat, n_lon, side),
                device_id_type=pl.DeviceIdType.MESH,
            )
        )
        copies[-1].start()
    return copies


def shifted_blocks():
    for si in range(SW_R):
        for sj in range(SW_C):
            for k in range(4):
                yield ((si * SW_C + sj) * 4 + k) * BLK, 2 * si - 1 + k // 2, 2 * sj - 1 + k % 2


def inside(bi, bj):
    return 0 <= bi < BR and 0 <= bj < BC


def outer(out_ref, halos):
    for n, (_, bi, bj) in enumerate(outer_blocks()):
        r = -1 if bi < 0 else 1 if bi >= BR else 0
        c = -1 if bj < 0 else 1 if bj >= BC else 0
        halo = halos[SIDES.index((r, c))]
        if c == 0:
            value = halo[bj // 2, bj % 2]
        elif r == 0:
            value = halo[bi // 2, bi % 2]
        else:
            value = halo[...]
        out_ref[pl.ds(n * BLK, BLK), :] = value


def outer_blocks():
    return [b for b in shifted_blocks() if not inside(b[1], b[2])]


TO = len(outer_blocks()) * BLK


FETCHED = ["values", "state", "wemb", "wqkv", "wproj", "wup", "wdown", "w1", "w2", "rinv", "whead", "background"]


def whole_kernel(
    n_lat, n_lon, count_ref, owner_ref, point_ref, gain_ref, scale_ref, order_ref, place_ref, pixel_ref, inverse_ref,
    *refs,
):
    n = len(FETCHED)
    source = dict(zip(FETCHED, refs[:n]))
    result = refs[n]
    refs = refs[n + 1 :]
    held = dict(zip(FETCHED, refs[: n - 1]))
    refs = refs[n - 1 :]
    n = 0
    (sb, h0, hm0, h1, hm1, z1, qkv0, qkv1, r0, r1, p0, p1, gp0, gp1, o, zo, qo, hot, adj, gm) = refs[n : n + 20]
    held["background"] = gm
    halo_z, halo_a = refs[n + 20 : n + 28], refs[n + 28 : n + 36]
    recv, recv_aux, send_aux, w1, fetch_sem, out_sem, send_z, recv_z, send_a, recv_a, sems = refs[n + 36 :]
    fetches = {name: pltpu.make_async_copy(source[name], held[name], fetch_sem.at[k]) for k, name in enumerate(FETCHED)}
    for name in FETCHED[:-1]:
        fetches[name].start()
    barrier = pltpu.get_barrier_semaphore()
    me = lax.axis_index("lat") * n_lon + lax.axis_index("lon")

    def greet(k, _):
        pl.semaphore_signal(
            barrier, inc=1, device_id=other(n_lon, lax.rem(me + k, DEV)), device_id_type=pl.DeviceIdType.MESH
        )
        return 0

    lax.fori_loop(1, DEV, greet, 0)
    ones32, ones64, hmask = same_group(D, D // HEADS), same_group(GROUP, WT), head_mask()
    log2e = 1.4426950408889634
    scale0, scale1 = scale_ref[0:1, :], scale_ref[1:2, :]
    plain = (1, list(range(T // WT)))
    shifted = (1, list(range(TX // WT)))

    fetches["values"].wait()
    pl.semaphore_wait(barrier, DEV - 1)
    kept = route(
        n_lon, me, owner_ref, point_ref, count_ref[0], held["values"], gm,
        adj.at[pl.ds(0, OBS), pl.ds(CHAN, CHAN)], adj, send_aux, recv, recv_aux, sems,
    )

    fetches["background"].start()

    perm = permutation(order_ref[...])
    fetches["state"].wait()
    sb[...] = held["state"][...].astype(BF16)
    fetches["wemb"].wait()
    fetches["wqkv"].wait()
    for i in range(T // ROWS):
        rows = pl.ds(i * ROWS, ROWS)
        mine = mm(perm[i * ROWS : (i + 1) * ROWS], sb[...]).astype(BF16)
        hidden = mm(mine, held["wemb"][...])
        h0[rows, :] = hidden
        qkv0[rows, :], r0[rows, :] = project(norm(hidden, gain_ref[0, 0:1, :]), held["wqkv"][0], ones32)

    def put_o(w, value):
        o[window(w), :] = value

    attend(plain, ROWS, qkv0, p0, scale0 * log2e, lambda n: None, put_o, hmask, ones64)
    fetches["wproj"].wait()
    fetches["wup"].wait()
    fetches["wdown"].wait()
    hm0[...] = h0[...] + mm(o[pl.ds(0, T), :], held["wproj"][0]).astype(BF16).astype(F32)

    def put_first(i, rows, value):
        h1[rows, :] = value
        put_packed(z1, i, norm(value, gain_ref[1, 0:1, :]))

    feed(hm0, gain_ref[0, 1:2, :], held["wup"].at[0], held["wdown"].at[0], gp0, put_first)

    copies = swap_edges(n_lat, n_lon, z1, halo_z, send_z, recv_z)
    lax.fori_loop(EARLY, SLOTS // CHUNK, functools.partial(send, n_lon, me, adj, recv, sems), 0)
    for i in range(T // ROWS):
        for k in range(ROWS // WT):
            w = i * (ROWS // WT) + k
            o[pl.ds(w * WT, WT), :] = z1[w // 6, w % 6].reshape(WT, D)
        rows = pl.ds(i * ROWS, ROWS)
        qo[rows, :], zo[rows, :] = project(o[rows, :], held["wqkv"][1], ones32)
    for row, bi, bj in shifted_blocks():
        if inside(bi, bj):
            qkv1[pl.ds(row, BLK), :] = qo[pl.ds(block_at(bi, bj), BLK), :]
            r1[pl.ds(row, BLK), :] = zo[pl.ds(block_at(bi, bj), BLK), :]
    for copy in copies:
        copy.wait()
    outer(o, halo_z)
    for i in range(2):
        rows = pl.ds(i * (TO // 2), TO // 2)
        qo[rows, :], _ = project(o[rows, :], held["wqkv"][1], ones32)
    for k, (row, _, _) in enumerate(outer_blocks()):
        qkv1[pl.ds(row, BLK), :] = qo[pl.ds(k * BLK, BLK), :]
    a = lax.broadcasted_iota(jnp.int32, (WT, GROUP), 0) // (2 * BLK)
    b = lax.broadcasted_iota(jnp.int32, (WT, GROUP), 1) // (2 * BLK) % 2
    apart = (a != b).astype(F32)
    lat = lax.axis_index("lat")
    top = 1.0 - apart * (lat == 0).astype(F32)
    bottom = 1.0 - apart * (lat == n_lat - 1).astype(F32)
    attend(shifted, TX // 3, qkv1, p1, scale1 * log2e, lambda n: (top, None, bottom)[n // SW_C], put_o, hmask, ones64)
    for row, bi, bj in shifted_blocks():
        if inside(bi, bj):
            zo[pl.ds(block_at(bi, bj), BLK), :D] = o[pl.ds(row, BLK), :]
    hm1[...] = h1[...] + mm(zo[:, :D], held["wproj"][1]).astype(BF16).astype(F32)

    def put_second(i, rows, value):
        zo[rows, :D] = value.astype(BF16)

    feed(hm1, gain_ref[1, 1:2, :], held["wup"].at[1], held["wdown"].at[1], gp1, put_second)
    back = permutation(place_ref[...])
    fetches["whead"].wait()
    for i in range(T // ROWS):
        rows = pl.ds(i * ROWS, ROWS)
        mine = mm(back[i * ROWS : (i + 1) * ROWS], zo[:, :D]).astype(BF16)
        sb[rows, :] = (held["state"][rows, :] + mm_nt(mine, held["whead"][...])).astype(BF16)

    for name in ("w1", "w2", "rinv", "background"):
        fetches[name].wait()
    value = lax.broadcasted_iota(jnp.int32, (PV, VARS), 0) % VARS
    copies = (value == lax.broadcasted_iota(jnp.int32, (PV, VARS), 1)).astype(BF16)
    w1[...] = mm(copies, held["w1"][...].astype(BF16)).astype(BF16)
    routed(kept, 1, recv_aux, sems)
    inner = adj.at[pl.ds(0, SLOTS), pl.ds(CHAN, CHAN)]
    numbers = recv_aux[:, 0, :].astype(BF16)
    radiance(numbers, sb, pixel_ref[...], w1, hot, inner)
    for i in range(T // ROWS):
        rows = pl.ds(i * ROWS, ROWS)
        gm[rows, :] = inverse_ref[...] * (held["state"][rows, :] - held["background"][rows, :])
    routed(kept, 0, recv, sems)
    radiance_back(numbers, recv, pixel_ref[...], w1, held["w2"][...], held["rinv"][...], inner, adj)
    for i in range(T // ROWS):
        rows = pl.ds(i * ROWS, ROWS)
        value = mm(hot[rows, :], adj[...])
        gm[rows, :] = gm[rows, :] + value
        zo[rows, :D] = mm(value.astype(BF16), held["whead"][...]).astype(BF16)

    perm = permutation(order_ref[...])
    for i in range(T // ROWS):
        rows = pl.ds(i * ROWS, ROWS)
        d3 = mm(perm[i * ROWS : (i + 1) * ROWS], zo[:, :D])
        d2 = feed_back(rows, d3, hm1, gain_ref[1, 1:2, :], held["wup"].at[1], held["wdown"].at[1], gp1)
        hm1[rows, :] = d2
        put_packed(z1, i, d2.astype(BF16))
    copies = swap_edges(n_lat, n_lon, z1, halo_a, send_a, recv_a)
    wp = held["wproj"][1]
    for w in range(T // WT):
        zo[pl.ds(w * WT, WT), :D] = z1[w // 6, w % 6].reshape(WT, D)
    zo[:, D:] = mm_nt(zo[:, :D], wp).astype(BF16)
    for row, bi, bj in shifted_blocks():
        if inside(bi, bj):
            o[pl.ds(row, BLK), :] = zo[pl.ds(block_at(bi, bj), BLK), D:]
    for copy in copies:
        copy.wait()
    outer(zo.at[:, :D], halo_a)
    zo[pl.ds(0, TO), D:] = mm_nt(zo[pl.ds(0, TO), :D], wp).astype(BF16)
    for k, (row, _, _) in enumerate(outer_blocks()):
        o[pl.ds(row, BLK), :] = zo[pl.ds(k * BLK, BLK), D:]
    whole_back(
        shifted, plain, ones32, ones64, hmask, scale0, scale1, gain_ref, held, h0, hm0, h1, hm1,
        qkv0, qkv1, r0, r1, p0, p1, gp0, o, zo, qo, adj,
    )
    back = permutation(place_ref[...])
    parts = []
    for i in range(T // ROWS):
        rows = pl.ds(i * ROWS, ROWS)
        d0 = mm(back[i * ROWS : (i + 1) * ROWS], zo[:, :D]).astype(BF16)
        gm[rows, :] = gm[rows, :] + mm_nt(d0, held["wemb"][...])
        parts.append(pltpu.make_async_copy(gm.at[rows], result.at[rows], out_sem.at[i]))
        parts[-1].start()
    for part in parts:
        part.wait()


def whole_back(
    shifted, plain, ones32, ones64, hmask, scale0, scale1, gain_ref, held, h0, hm0, h1, hm1,
    qkv0, qkv1, r0, r1, p0, p1, gp0, o, zo, qo, adj,
):
    ds = adj.at[pl.ds(0, TX), pl.ds(0, 2 * GROUP)]
    dqkv = adj.at[pl.ds(TX, TX), pl.ds(0, 3 * D)]
    attend_back(shifted, TX // 3, qkv1, p1, o, ds, dqkv, scale1, hmask, ones64)
    step = TX // 3
    for i in range(3):
        rows = pl.ds(i * step, step)
        dqkv[rows, :] = through_unit(dqkv[rows, :], qkv1[rows, :], r1[rows, :], ones32)
    for row, bi, bj in shifted_blocks():
        if inside(bi, bj):
            qo[pl.ds(block_at(bi, bj), BLK), :] = dqkv[pl.ds(row, BLK), :]
    for i in range(T // ROWS):
        rows = pl.ds(i * ROWS, ROWS)
        dz = mm_nt(qo[rows, :], held["wqkv"][1])
        d1 = hm1[rows, :] + norm_back(h1[rows, :], gain_ref[1, 0:1, :], dz)
        dm = feed_back(rows, d1, hm0, gain_ref[0, 1:2, :], held["wup"].at[0], held["wdown"].at[0], gp0)
        hm1[rows, :] = dm
        o[rows, :] = mm_nt(dm.astype(BF16), held["wproj"][0]).astype(BF16)
    attend_back(plain, ROWS, qkv0, p0, o, ds, dqkv, scale0, hmask, ones64)
    for i in range(T // ROWS):
        rows = pl.ds(i * ROWS, ROWS)
        dz = mm_nt(through_unit(dqkv[rows, :], qkv0[rows, :], r0[rows, :], ones32), held["wqkv"][0])
        zo[rows, :D] = (hm1[rows, :] + norm_back(h0[rows, :], gain_ref[0, 0:1, :], dz)).astype(BF16)


STEP = 512


def numbers_of(numbers, i):
    slot = lax.broadcasted_iota(jnp.int32, (STEP, DEV), 0)
    across = lax.broadcasted_iota(jnp.int32, (STEP, DEV), 1)
    kinds = (
        lax.broadcasted_iota(jnp.int32, (DEV, DEV), 0) // CAP == lax.broadcasted_iota(jnp.int32, (DEV, DEV), 1)
    ).astype(BF16)
    sender = (slot // CAP + i * (STEP // CAP) == across).astype(BF16)
    mine = jnp.where(across % CAP == slot % CAP, mm(sender, numbers), 0.0)
    return mm(mine.astype(BF16), kinds)


def in_pairs(chunk):
    def chunks(i, _):
        chunk(2 * i)
        chunk(2 * i + 1)
        return 0

    lax.fori_loop(0, SLOTS // STEP // 2, chunks, 0)


def radiance(numbers, moved_ref, pixel, w1_ref, hot_ref, inner_ref):
    eye = (
        lax.broadcasted_iota(jnp.int32, (16, DEV), 0) == lax.broadcasted_iota(jnp.int32, (16, DEV), 1)
    ).astype(BF16)
    lane = lax.broadcasted_iota(jnp.int32, (STEP, T), 1)
    row = lax.broadcasted_iota(jnp.int32, (T, STEP), 0)

    def chunk(i):
        rows = pl.ds(pl.multiple_of(i * STEP, STEP), STEP)
        aux = numbers_of(numbers, i)
        flat = mm_nt(eye, aux.astype(BF16))
        patch = jnp.where(aux[:, 3:4] > 0, aux[:, 0:1] * PIX + aux[:, 1:2], -1.0).astype(jnp.int32)
        hot = (lane == patch).astype(BF16)
        patches = jnp.where(flat[3:4] > 0, flat[0:1] * PIX + flat[1:2], -1.0).astype(jnp.int32)
        hot_ref[:, rows] = (row == patches).astype(BF16)
        found = jnp.where(pixel == aux[:, 2:3], mm(hot, moved_ref[...]), 0.0).astype(BF16)
        inner_ref[rows, :] = jnp.tanh(mm(found, w1_ref[...])).astype(BF16)

    in_pairs(chunk)


def radiance_back(numbers, recv_ref, pixel, w1_ref, w2, rinv, inner_ref, adj_ref):
    w2, rinv = w2.astype(BF16), rinv.astype(BF16)

    def chunk(i):
        rows = pl.ds(pl.multiple_of(i * STEP, STEP), STEP)
        aux = numbers_of(numbers, i)
        inner16 = inner_ref[rows, :]
        inner = inner16.astype(F32)
        observed = recv_ref[pl.ds(i * (STEP // CAP), STEP // CAP)].reshape(STEP, CHAN)
        innovation = (mm(inner16, w2) - observed.astype(F32)) * aux[:, 3:4]
        weighted = mm(innovation.astype(BF16), rinv).astype(BF16)
        pulled = mm_nt(weighted, w2) * (1.0 - inner * inner)
        adj = mm_nt(pulled.astype(BF16), w1_ref[...])
        adj_ref[rows, :] = jnp.where(pixel == aux[:, 2:3], adj, 0.0).astype(BF16)

    in_pairs(chunk)


def whole(n_lat, n_lon, small, fetched):
    halo = [pltpu.VMEM(s + (BLK, D), BF16) for s in SHAPES]
    ANY = pl.BlockSpec(memory_space=pl.ANY)
    scratch = [pltpu.VMEM(a.shape, a.dtype) for a in fetched[:-1]]
    scratch += [
        pltpu.VMEM(s, d)
        for s, d in [
            ((T, PV), BF16), ((T, D), F32), ((T, D), F32), ((T, D), F32), ((T, D), F32), (PACKED, BF16),
            ((T, 3 * D), BF16), ((TX, 3 * D), BF16), ((T, 2 * D), BF16), ((TX, 2 * D), BF16),
            ((T, 2 * GROUP), BF16), ((TX, 2 * GROUP), BF16), ((T, FFN), BF16), ((T, FFN), BF16),
            ((TX, D), BF16), ((T, 2 * D), BF16), ((T, 3 * D), BF16),
            ((T, SLOTS), BF16), ((SLOTS, PV), BF16), ((T, PV), F32),
        ]
    ]
    scratch += halo + halo
    scratch += [
        pltpu.VMEM((DEV, CAP, CHAN), BF16), pltpu.VMEM((DEV, 1, DEV), F32), pltpu.VMEM((DEV, 1, DEV), F32),
        pltpu.VMEM((PV, D), BF16),
    ]
    scratch += [pltpu.SemaphoreType.DMA((len(fetched),)), pltpu.SemaphoreType.DMA((T // ROWS,))]
    scratch += [pltpu.SemaphoreType.DMA((8,))] * 4 + [pltpu.SemaphoreType.DMA((6,))]
    return pl.pallas_call(
        functools.partial(whole_kernel, n_lat, n_lon),
        out_shape=jax.ShapeDtypeStruct((T, PV), F32),
        in_specs=[SMEM] + [VMEM] * (len(small) - 1) + [ANY] * len(fetched),
        out_specs=ANY,
        scratch_shapes=scratch,
        compiler_params=pltpu.CompilerParams(vmem_limit_bytes=62 << 20, collective_id=1, has_side_effects=True),
    )(*small, *fetched)


def local(
    n_lat, n_lon, state, background, inv_background, w_embed, norm_gain, w_qkv, w_proj, head_scale, w_up,
    w_down, w_head, w_obs1, w_obs2, r_inverse, obs_values, obs_owner, obs_point, obs_count,
):
    order = jnp.asarray(ORDER).reshape(T, 1)
    place = jnp.asarray(PLACE).reshape(T, 1)
    scales = jnp.repeat(head_scale, WT, axis=1)
    pixel = (jnp.arange(PV, dtype=jnp.int32) // VARS).astype(F32).reshape(1, PV)
    small = [
        obs_count, obs_owner.reshape(1, OBS), obs_point.reshape(1, OBS), norm_gain, scales, order, place, pixel,
        inv_background.reshape(1, PV),
    ]
    fetched = [
        obs_values, state.reshape(T, PV), w_embed, w_qkv, w_proj, w_up, w_down, w_obs1, w_obs2, r_inverse, w_head.T,
        background.reshape(T, PV),
    ]
    return whole(n_lat, n_lon, small, fetched).reshape(state.shape)


def solution(mesh):
    grid = P("lat", "lon", None)
    slots = P(("lat", "lon"))
    placed = (grid, grid) + (P(),) * 12 + (P(("lat", "lon"), None),) * 2 + (slots, slots)
    return jax.shard_map(
        functools.partial(local, mesh.shape["lat"], mesh.shape["lon"]),
        mesh=mesh,
        in_specs=placed,
        out_specs=grid,
        check_vma=False,
    )
```
